256 devices in a mesh: ctx: 8 (over x, core), lang: 32 (over z, y).
Axes of the slice: x: 4, y: 4, z: 8, core: 2. Of those that a mesh axis runs over, the one named last changes fastest.
Arguments:
- attn_queries: bfloat16 [32, 1024, 1024], P('lang', 'ctx'), may hold values from -100 to 100
- attn_keys: bfloat16 [32, 1024, 1024], P('lang', 'ctx'), may hold values from -5 to 5
- attn_values: bfloat16 [32, 1024, 1024], P('lang', 'ctx'), may hold values from -6 to 6
- residual: bfloat16 [32, 1024, 1024], P('lang', 'ctx'), may hold values from -6 to 6
- cotangent: bfloat16 [32, 1024, 1024], P('lang', 'ctx'), may hold values from -6 to 6
- segment_ids: int32 [32, 1024], P('lang', 'ctx'), may hold values from 0 to 7, never falling along the last dimension, each value on 1 to 512 neighbouring positions
- language_ids: int32 [32, 1024, 1], P('lang', 'ctx'), may hold values from 0 to 31; in each aligned block of 128 rows (0 to 127, 128 to 255, ..., all dimensions but the last counted through in order) at most 5 rows name the same one
- token_counts: int32 [32], replicated, may hold values from 16 to 1023
- norm_gain: float32 [1024], replicated, may hold values from 0.1 to 1.9
- gate_weight: bfloat16 [32, 1024, 4096], P('lang', None, 'ctx'), may hold values from -0.1875 to 0.1875
- up_weight: bfloat16 [32, 1024, 4096], P('lang', None, 'ctx'), may hold values from -0.1875 to 0.1875
- down_weight: bfloat16 [32, 4096, 1024], P('lang', 'ctx'), may hold values from -0.09375 to 0.09375
Outputs:
- layer_out: bfloat16 [32, 1024, 1024], P('lang', 'ctx')
- grad_queries: bfloat16 [32, 1024, 1024], P('lang', 'ctx')
- grad_keys: bfloat16 [32, 1024, 1024], P('lang', 'ctx')
- grad_values: bfloat16 [32, 1024, 1024], P('lang', 'ctx')
- grad_residual: bfloat16 [32, 1024, 1024], P('lang', 'ctx')
- grad_gain: float32 [1024], replicated
- grad_gate: bfloat16 [32, 1024, 4096], P('lang', None, 'ctx')
- grad_up: bfloat16 [32, 1024, 4096], P('lang', None, 'ctx')
- grad_down: bfloat16 [32, 4096, 1024], P('lang', 'ctx')
The draws below stay inside these ranges and needn't reach their ends.
Inputs may be any that keep to these rules, and one draw needn't show every extreme that they name: `language_ids`: in each aligned block of 128 positions (the positions of one device) no language is named by more than 5 positions, a bound that some block reaches. `segment_ids`: never falling along a sequence; each document holds 1 to 512 positions.
All inputs are finite; a program needn't handle non-finite values.
Results may differ from the reference program's by a relative error of at most 0.023.
Values may be sent and summed in bfloat16 or wider, within the bound.
A program may use at most 128 MiB of HBM per device.

```python
import math
import jax
import jax.numpy as jnp
import numpy as np
from jax import lax

D = 1024
HEADS = 8
HD = 128
FF = 4096
TOK_DEV = 128
DOCS = 8
LEN = 1024
SEQS = 32
LANGS = 32
CAP = 5
N_CTX = 8
N_LANG = 32


def shared_keys(key):
    return jnp.clip(jax.random.normal(key, (SEQS, LEN, D), jnp.float32), -5.0, 5.0)


def draw_attn_keys(key, part):
    shared = shared_keys(key)
    return shared.astype(jnp.bfloat16)


def draw_attn_queries(key, part):
    key = jax.random.fold_in(key, 5)
    own_rows = jnp.clip(jax.random.normal(key, (SEQS, LEN, D), jnp.float32), -5.0, 5.0)
    return own_rows.astype(jnp.bfloat16)


def set_ends(drawn, stream_key, least, top_value):
    longest = drawn.shape.index(max(drawn.shape))
    spots = []
    for shift in (0, 1):
        where = [jax.random.randint(jax.random.fold_in(stream_key, axis), (), 0, length) for axis, length in enumerate(drawn.shape)]
        where[longest] = (where[longest] + shift) % drawn.shape[longest]
        spots.append(tuple(where))
    return drawn.at[spots[0]].set(least).at[spots[1]].set(top_value)


def shard_levels(key, dims, pieces, least, largest):
    def one(axis_at, blocks):
        draws = jax.random.uniform(jax.random.fold_in(jax.random.fold_in(key, 6), axis_at), (blocks,), jnp.float32, least / len(pieces), largest / len(pieces))
        return jnp.repeat(jnp.exp(draws), dims[axis_at] // blocks).reshape((-1,) + (1,) * (len(dims) - axis_at - 1))

    gain = one(*pieces[0])
    for cut in pieces[1:]:
        gain = gain * one(*cut)
    return gain


def split_up(amount, total, reach, slope):
    weights = [(1 << 20) // math.isqrt(grade ** slope) + 1 for grade in range(2, amount + 1)]
    spare, holding = total - reach - (amount - 1), [1] * (amount - 1)
    while spare > 0:
        free = [i for i in range(amount - 1) if holding[i] < reach]
        pool, budget = sum([weights[i] for i in free]), spare
        for i in free:
            extra = min(reach - holding[i], max(1, budget * weights[i] // pool), spare)
            holding[i] = holding[i] + extra
            spare = spare - extra
    return np.array([reach] + holding)


def uneven_parts(stream_key, count, total, most, slope):
    if count == 2:
        one = jax.random.randint(stream_key, (), max(1, total - most), min(most, total - 1) + 1)
        return jnp.stack([one, total - one])
    sizes = jnp.asarray(split_up(count, total, most, slope), jnp.int32)
    twos = (count - 1) // 2
    giver, receiver = sizes[1:1 + 2 * twos:2], sizes[2:2 + 2 * twos:2]
    slack = jnp.minimum(giver - 1, most - receiver)
    moved = jax.random.randint(jax.random.fold_in(stream_key, 1), (twos,), 0, 1 << 20) % (slack + 1)
    sizes = sizes.at[1:1 + 2 * twos:2].set(giver - moved).at[2:2 + 2 * twos:2].set(receiver + moved)
    return sizes[jax.random.permutation(jax.random.fold_in(stream_key, 2), count)]


def routed_block(own_key, own, number, rows, count, top, bound, slope):
    order = jax.random.permutation(own_key, count)
    crowded, common = portions_of(count, rows * top, bound, slope, True), portions_of(count, rows * top, bound, slope, False)
    places = jnp.arange(count)

    def named(lengths, turn):
        used = int((lengths > 0).sum())
        fixed = max(1, used // 4)
        moved = fixed + (places - fixed + turn * (used - fixed)) % max(1, count - fixed)
        return jnp.zeros((count,), jnp.int32).at[order[jnp.where(places < fixed, places, moved)]].set(jnp.asarray(lengths, jnp.int32))

    lengths = jnp.where(number % 4 == 0, named(crowded, number // 4), named(common, number - number // 4 - 1))
    mixed = jax.random.permutation(jax.random.fold_in(own, 3), count)
    source_of, sink = mixed[0:count // 2 * 2:2], mixed[1:count // 2 * 2:2]
    room = jnp.minimum(lengths[source_of] - 1, bound - lengths[sink]) // 2
    room = jnp.where((source_of == order[0]) | (sink == order[0]) | (lengths[sink] == 0), 0, jnp.maximum(room, 0))
    moved = jax.random.randint(jax.random.fold_in(own, 4), (count // 2,), 0, 1 << 20) % (room + 1)
    lengths = lengths.at[source_of].add(-moved).at[sink].add(moved)
    members = jnp.searchsorted(jnp.cumsum(lengths), jnp.arange(rows * top), side="right").astype(jnp.int32)
    grid = members.reshape(top, rows).T
    grid = grid[jax.random.permutation(jax.random.fold_in(own, 1), rows)]
    turn = jax.random.randint(jax.random.fold_in(own, 2), (rows, 1), 0, top)
    return jnp.take_along_axis(grid, (jnp.arange(top)[None, :] + turn) % top, axis=1)


def portions_of(count, total, bound, slope, full):
    weights = [(1 << 20) // math.isqrt(grade ** slope) + 1 for grade in range(1, count + 1)]
    largest = bound if full else min(bound, max(-(-total // count), total * weights[0] // sum(weights)))
    least = 1 if total - largest >= count - 1 else 0
    counts, rest = [largest] + [least] * (count - 1), total - largest - least * (count - 1)
    while rest > 0:
        free = [i for i in range(1, count) if counts[i] < largest] or [i for i in range(1, count) if counts[i] < bound]
        whole, budget = sum([weights[i] for i in free]), rest
        for i in free:
            extra = min(bound - counts[i], max(1, budget * weights[i] // whole), rest)
            counts[i] = counts[i] + extra
            rest = rest - extra
    return np.array(counts)


def noise(rng, extent, spread, limit, shards=(), held_as=jnp.bfloat16):
    values = jax.random.normal(rng, extent, jnp.float32) * spread
    if len(shards) > 0:
        values = shard_levels(rng, extent, shards, -0.22, 0.18) * values
    return jnp.clip(values, min=-limit, max=limit).astype(held_as)


def setup_inputs(seed: int = 0) -> dict:
    key_of = jax.random.split(jax.random.key(seed), 13)
    attn_queries = draw_attn_queries(jax.random.fold_in(key_of[12], 71), 0)
    attn_keys = draw_attn_keys(jax.random.fold_in(key_of[12], 71), 0)
    attn_values = noise(key_of[2], (SEQS, LEN, D), 1.0, 6.0, ((0, 32), (1, 8)))
    residual = noise(key_of[3], (SEQS, LEN, D), 1.0, 6.0, ((0, 32), (1, 8)))
    cotangent = noise(key_of[4], (SEQS, LEN, D), 1.0, 6.0, ((0, 32), (1, 8)))
    segment_ids = jax.vmap(lambda own: jnp.searchsorted(jnp.cumsum(uneven_parts(own, DOCS, LEN, LEN // 2, 0)), jnp.arange(LEN), side="right"))(jax.random.split(key_of[5], SEQS)).reshape((SEQS, LEN)).astype(jnp.int32)
    language_ids_keys = jax.random.split(jax.random.fold_in(key_of[6], 1), SEQS * LEN // TOK_DEV)
    language_ids_turns = jax.random.permutation(jax.random.fold_in(key_of[6], 3), SEQS * LEN // TOK_DEV)
    language_ids = jax.vmap(lambda own, number: routed_block(jax.random.fold_in(key_of[6], 2), own, number, TOK_DEV, LANGS, 1, CAP, 2))(language_ids_keys, language_ids_turns).reshape((SEQS, LEN, 1))
    token_counts = set_ends(jax.random.randint(key_of[7], (LANGS,), 16, 1024), jax.random.fold_in(key_of[7], 1), 16, 1023).astype(jnp.int32)
    norm_gain = jnp.clip(1.0 + 0.18 * jax.random.normal(key_of[8], (D,), jnp.float32), 0.1, 1.9)
    gate_weight = noise(key_of[9], (LANGS, D, FF), D ** -0.5, 0.1875, ((0, 32), (2, 8)))
    up_weight = noise(key_of[10], (LANGS, D, FF), D ** -0.5, 0.1875, ((0, 32), (2, 8)))
    down_weight = noise(key_of[11], (LANGS, FF, D), FF ** -0.5, 0.09375, ((0, 32), (1, 8)))
    return {"attn_queries": attn_queries, "attn_keys": attn_keys, "attn_values": attn_values, "residual": residual, "cotangent": cotangent, "segment_ids": segment_ids, "language_ids": language_ids, "token_counts": token_counts, "norm_gain": norm_gain, "gate_weight": gate_weight, "up_weight": up_weight, "down_weight": down_weight}


EPSILON = 1e-06

def probs_of(query_heads, key_heads, seg_row, score_scale):
    scores = jnp.einsum('qhd,khd->hqk', query_heads.astype(jnp.float32), key_heads.astype(jnp.float32)) * score_scale
    allowed = seg_row[:, None] == seg_row[None, :]
    scores = jnp.where(allowed[None], scores, -jnp.inf)
    top_score = lax.optimization_barrier(jnp.max(scores, axis=-1, keepdims=True))
    exp_terms = jnp.exp(scores - top_score)
    return exp_terms / lax.optimization_barrier(jnp.sum(exp_terms, axis=-1, keepdims=True))

def attend_sequence(packed):
    query_rows, key_rows, value_rows, seg_row = packed
    score_scale = HD ** (-0.5)
    query_heads = query_rows.reshape(LEN, HEADS, HD)
    key_heads = key_rows.reshape(LEN, HEADS, HD)
    value_heads = value_rows.reshape(LEN, HEADS, HD)
    attn_probs = probs_of(query_heads, key_heads, seg_row, score_scale)
    probs_half = attn_probs.astype(jnp.bfloat16)
    attended = jnp.einsum('hqk,khd->qhd', probs_half.astype(jnp.float32), value_heads.astype(jnp.float32))
    return attended.astype(jnp.bfloat16).reshape(LEN, D)

def attend_backward(packed):
    query_rows, key_rows, value_rows, seg_row, grad_rows = packed
    score_scale = HD ** (-0.5)
    query_heads = query_rows.reshape(LEN, HEADS, HD)
    key_heads = key_rows.reshape(LEN, HEADS, HD)
    value_heads = value_rows.reshape(LEN, HEADS, HD)
    attn_probs = probs_of(query_heads, key_heads, seg_row, score_scale)
    probs_half = attn_probs.astype(jnp.bfloat16)
    grad_heads = grad_rows.reshape(LEN, HEADS, HD).astype(jnp.float32)
    grad_value = jnp.einsum('hqk,qhd->khd', probs_half.astype(jnp.float32), grad_heads).astype(jnp.bfloat16)
    grad_probs = jnp.einsum('qhd,khd->hqk', grad_heads, value_heads.astype(jnp.float32))
    grad_scores = (attn_probs * (grad_probs - lax.optimization_barrier(jnp.sum(attn_probs * grad_probs, axis=-1, keepdims=True)))).astype(jnp.bfloat16)
    grad_query = (jnp.einsum('hqk,khd->qhd', grad_scores.astype(jnp.float32), key_heads.astype(jnp.float32)) * score_scale).astype(jnp.bfloat16)
    grad_key = (jnp.einsum('hqk,qhd->khd', grad_scores.astype(jnp.float32), query_heads.astype(jnp.float32)) * score_scale).astype(jnp.bfloat16)
    return (grad_query.reshape(LEN, D), grad_key.reshape(LEN, D), grad_value.reshape(LEN, D))

def reference(attn_queries, attn_keys, attn_values, residual, cotangent, segment_ids, language_ids, token_counts, norm_gain, gate_weight, up_weight, down_weight):
    attended = lax.map(attend_sequence, (attn_queries, attn_keys, attn_values, segment_ids))
    summed = residual.astype(jnp.float32) + attended.astype(jnp.float32)
    inv_rms = lax.rsqrt(lax.optimization_barrier(jnp.mean(summed * summed, axis=-1, keepdims=True)) + EPSILON)
    normed = summed * inv_rms
    normin = (normed * norm_gain).astype(jnp.bfloat16)
    lang_flat = language_ids.reshape(-1).astype(jnp.int32)
    tok_weight = (16.0 * lax.rsqrt(token_counts[lang_flat].astype(jnp.float32))).reshape(SEQS, LEN, 1)
    grad_out = cotangent.astype(jnp.float32) * tok_weight
    grad_ffn = grad_out.astype(jnp.bfloat16)
    normin_flat = normin.reshape(-1, D)
    grad_flat = grad_ffn.reshape(-1, D)
    row_limit = N_CTX * N_LANG * CAP

    def language_block(language):
        member = lang_flat == language
        total = jnp.sum(member.astype(jnp.int32))
        positions = jnp.nonzero(member, size=row_limit, fill_value=0)[0].astype(jnp.int32)
        valid = (jnp.arange(row_limit, dtype=jnp.int32) < total)[:, None]
        rows_in = jnp.where(valid, normin_flat[positions], jnp.zeros((), jnp.bfloat16))
        grad_in = jnp.where(valid, grad_flat[positions], jnp.zeros((), jnp.bfloat16))
        w_gate = lax.dynamic_index_in_dim(gate_weight, language, 0, keepdims=False)
        w_up = lax.dynamic_index_in_dim(up_weight, language, 0, keepdims=False)
        w_down = lax.dynamic_index_in_dim(down_weight, language, 0, keepdims=False)
        pre_gate = jnp.dot(rows_in, w_gate, preferred_element_type=jnp.float32)
        pre_up = jnp.dot(rows_in, w_up, preferred_element_type=jnp.float32)
        sigmoid_gate = jax.nn.sigmoid(pre_gate)
        silu_gate = pre_gate * sigmoid_gate
        hidden = (silu_gate * pre_up).astype(jnp.bfloat16)
        ffn_rows = jnp.dot(hidden, w_down, preferred_element_type=jnp.float32).astype(jnp.bfloat16)
        grad_hidden = jnp.dot(grad_in, w_down.T, preferred_element_type=jnp.float32)
        grad_down = jnp.dot(hidden.T, grad_in, preferred_element_type=jnp.float32).astype(jnp.bfloat16)
        grad_gate_pre = (grad_hidden * pre_up * sigmoid_gate * (1.0 + pre_gate * (1.0 - sigmoid_gate))).astype(jnp.bfloat16)
        grad_up_pre = (grad_hidden * silu_gate).astype(jnp.bfloat16)
        grad_gate = jnp.dot(rows_in.T, grad_gate_pre, preferred_element_type=jnp.float32).astype(jnp.bfloat16)
        grad_up = jnp.dot(rows_in.T, grad_up_pre, preferred_element_type=jnp.float32).astype(jnp.bfloat16)
        grad_normin = (jnp.dot(grad_gate_pre, w_gate.T, preferred_element_type=jnp.float32) + jnp.dot(grad_up_pre, w_up.T, preferred_element_type=jnp.float32)).astype(jnp.bfloat16)
        ffn_kept = jnp.where(valid, ffn_rows.astype(jnp.float32), jnp.zeros((), jnp.float32))
        grad_kept = jnp.where(valid, grad_normin.astype(jnp.float32), jnp.zeros((), jnp.float32))
        return (ffn_kept, grad_kept, grad_gate, grad_up, grad_down, positions)
    ffn_all, grad_all, grad_gate, grad_up, grad_down, position_all = lax.map(language_block, jnp.arange(LANGS, dtype=jnp.int32))
    flat_index = position_all.reshape(-1)
    ffn_tok = jnp.zeros((SEQS * LEN, D), jnp.float32).at[flat_index].add(ffn_all.reshape(-1, D)).reshape(SEQS, LEN, D)
    grad_normin_tok = jnp.zeros((SEQS * LEN, D), jnp.float32).at[flat_index].add(grad_all.reshape(-1, D)).reshape(SEQS, LEN, D)
    layer_out = (summed + ffn_tok).astype(jnp.bfloat16)
    grad_gain = lax.optimization_barrier(jnp.sum(grad_normin_tok * normed, axis=(0, 1)))
    scaled = grad_normin_tok * norm_gain
    grad_residual = (grad_out + inv_rms * (scaled - normed * lax.optimization_barrier(jnp.mean(scaled * normed, axis=-1, keepdims=True)))).astype(jnp.bfloat16)
    grad_queries, grad_keys, grad_values = lax.map(attend_backward, (attn_queries, attn_keys, attn_values, segment_ids, grad_residual))
    return (layer_out, grad_queries, grad_keys, grad_values, grad_residual, grad_gain, grad_gate, grad_up, grad_down)
```

```python
import functools

import jax
import jax.numpy as jnp
from jax import lax
from jax.experimental import pallas as pl
from jax.experimental.pallas import tpu as pltpu
from jax.sharding import PartitionSpec as P

HD = 128
EPSILON = 1e-06
CAP = 5
PITCH = 6
GROUPS = 2
MESH = pl.DeviceIdType.MESH
F32 = jnp.float32
BF16 = jnp.bfloat16
MASKED = -1e30


def dot_nn(a, b):
    return lax.dot_general(a, b, (((1,), (0,)), ((), ())), preferred_element_type=F32)


def dot_nt(a, b):
    return lax.dot_general(a, b, (((1,), (1,)), ((), ())), preferred_element_type=F32)


def at(start, size, step=None):
    return pl.ds(pl.multiple_of(start, step or size), size)


def kernel(
    nctx,
    nlang,
    q_hbm,
    k_hbm,
    v_hbm,
    residual,
    cotangent,
    segment,
    language,
    counts,
    gain,
    wg_hbm,
    wu_hbm,
    wd_hbm,
    layer_out,
    gq_hbm,
    gk_hbm,
    gv_hbm,
    grad_res,
    grad_gain,
    gwg_hbm,
    gwu_hbm,
    gwd_hbm,
    qh,
    kh,
    vh,
    segsend,
    segrow,
    segcol,
    probs_t,
    attsend,
    att,
    wg,
    wu,
    wd,
    gwg,
    gwu,
    gwd,
    summed_s,
    normed_s,
    gout_s,
    gn_s,
    stack,
    sel,
    sel_t,
    spread,
    spread_t,
    stack_r,
    msg_s,
    msg_r,
    rows_n,
    rows_g,
    gh_s,
    hid_s,
    ggp_s,
    gup_s,
    part,
    pair_r,
    sum_s,
    fin_r,
    grsend,
    grh,
    gqsend,
    gk_acc,
    gv_acc,
    gksend,
    gvsend,
    gain_s,
    gain_c,
    gain_l_s,
    gain_l,
    loc_sem,
    out_sem,
    in_s,
    in_r,
    att_ss,
    att_rs,
    lang_ss,
    lang_rs,
    ag_ss,
    ag_fs,
    ag_rs,
    pair_ss,
    pair_rs,
    fin_ss,
    fin_rs,
    gr_ss,
    gr_rs,
    go_ss,
    go_rs,
    gain_ss,
    gain_rs,
    gainl_ss,
    gainl_rs,
):
    T, D = residual.shape
    L = nctx * T
    J = D // HD
    X = nctx // 2
    F = wg.shape[1]
    MR = PITCH * J
    LG = nlang // GROUPS
    RG = LG * CAP
    BR = nlang * CAP
    OP = 128
    scale = HD ** (-0.5)
    c = lax.axis_index("ctx")
    me = lax.axis_index("lang")
    x = c // 2
    core = c % 2
    sib = x * 2 + 1 - core

    def rcopy(src, dst, ssem, rsem, dev):
        return pltpu.make_async_remote_copy(
            src_ref=src, dst_ref=dst, send_sem=ssem, recv_sem=rsem, device_id=dev, device_id_type=MESH
        )

    def loop(lo, hi, body):
        def step(i, carry):
            body(i)
            return carry

        lax.fori_loop(lo, hi, step, 0)

    weight_in = [
        pltpu.make_async_copy(src, dst, loc_sem.at[i])
        for i, (src, dst) in enumerate(((wd_hbm, wd), (wg_hbm, wg), (wu_hbm, wu)))
    ]
    own_in = [
        pltpu.make_async_copy(src.at[:, at(c * HD, HD)], dst.at[at(c * T, T)], loc_sem.at[3 + i])
        for i, (src, dst) in enumerate(((k_hbm, kh), (q_hbm, qh), (v_hbm, vh)))
    ]
    segsend[...] = jnp.broadcast_to(segment[...].astype(F32), segsend.shape).astype(BF16)

    barrier = pltpu.get_barrier_semaphore()
    loop(1, nctx, lambda i: pl.semaphore_signal(barrier, inc=1, device_id={"ctx": (c + i) % nctx}, device_id_type=MESH))
    loop(1, nlang, lambda i: pl.semaphore_signal(barrier, inc=1, device_id={"lang": (me + i) % nlang}, device_id_type=MESH))
    for copy in own_in:
        copy.start()
    pl.semaphore_wait(barrier, nctx - 1 + nlang - 1)

    def in_copies(to, owner, sem_at):
        out = [
            rcopy(src.at[:, at(to * HD, HD)], dst.at[at(owner * T, T)], in_s.at[i, sem_at], in_r.at[i, owner], {"ctx": to})
            for i, (src, dst) in enumerate(((k_hbm, kh), (q_hbm, qh), (v_hbm, vh)))
        ]
        out.append(rcopy(segsend, segrow.at[:, at(owner * T, T)], in_s.at[3, sem_at], in_r.at[3, owner], {"ctx": to}))
        return out

    def send_in(i):
        to = (c + i) % nctx
        for copy in in_copies(to, c, to):
            copy.start()

    loop(1, nctx, send_in)
    for copy in weight_in:
        copy.start()
    segrow[:, at(c * T, T)] = segsend[...]

    lang_row = language[...].astype(F32)
    lang_col = jnp.transpose(jnp.broadcast_to(lang_row, (T, T)))
    earlier = lax.broadcasted_iota(jnp.int32, (T, T), 0) < lax.broadcasted_iota(jnp.int32, (T, T), 1)
    rank = jnp.sum(jnp.where((lang_col == lang_row) & earlier, 1.0, 0.0), axis=0, keepdims=True)
    slot_row = lang_row * float(MR) + rank
    slot_col = jnp.transpose(jnp.broadcast_to(slot_row, (T, T)))[:, 0:1].astype(jnp.int32)
    slot_row = slot_row.astype(jnp.int32)
    for j in range(J):
        hit = lax.broadcasted_iota(jnp.int32, (nlang * MR, T), 0) == slot_row + PITCH * j
        sel[:, j * T : (j + 1) * T] = jnp.where(hit, 1.0, 0.0).astype(BF16)

    lang_hit = lang_col[:, 0:1] == lax.broadcasted_iota(jnp.int32, (T, nlang), 1).astype(F32)
    count = jnp.sum(jnp.where(lang_hit, counts[...].astype(F32), 0.0), axis=1, keepdims=True)
    gout_s[...] = cotangent[...].astype(F32) * (16.0 * lax.rsqrt(count))

    def dispatch(phase, stacked):
        for j in range(J):
            stack[j * T : (j + 1) * T, :] = stacked[:, j * HD : (j + 1) * HD]
        msg_s[phase] = dot_nn(sel[...], stack[...]).astype(BF16)

        def one(d):
            to = (me + d) % nlang
            rcopy(
                msg_s.at[phase, at(to * MR, MR)],
                msg_r.at[phase, at(d * MR, MR)],
                lang_ss.at[phase, d],
                lang_rs.at[phase, d],
                {"lang": to},
            ).start()

        loop(1, nlang, one)
        msg_r[phase, 0:MR, :] = msg_s[phase, at(me * MR, MR), :]

    def lang_wait(phase, lo, hi):
        def one(d):
            rcopy(
                msg_s.at[phase, at(d * MR, MR)],
                msg_r.at[phase, at(d * MR, MR)],
                lang_ss.at[phase, d],
                lang_rs.at[phase, d],
                {"lang": me},
            ).wait_recv()

        loop(lo, hi, one)

    def lang_wait_but_own(phase):
        def one(d):
            l = (me + d) % nlang
            rcopy(
                msg_s.at[phase, at(l * MR, MR)],
                msg_r.at[phase, at(l * MR, MR)],
                lang_ss.at[phase, d],
                lang_rs.at[phase, l],
                {"lang": me},
            ).wait_recv()

        loop(1, nlang, one)

    dispatch(0, gout_s[...].astype(BF16))

    o_col = lax.broadcasted_iota(jnp.int32, (RG, LG * MR), 0)
    base = ((o_col * 205) >> 10) * (MR - CAP) + o_col
    for j in range(J):
        hit = lax.broadcasted_iota(jnp.int32, (RG, LG * MR), 1) == base + PITCH * j
        spread[j * RG : (j + 1) * RG, :] = jnp.where(hit, 1.0, 0.0).astype(BF16)

    for copy in own_in:
        copy.wait()

    def wait_in(i):
        for copy in in_copies((c + i) % nctx, (c + i) % nctx, (c + i) % nctx):
            copy.wait_recv()

    loop(1, nctx, wait_in)
    for p in range(nctx):
        row = segrow[0:1, p * T : (p + 1) * T].astype(F32)
        segcol[p * T : (p + 1) * T, :] = jnp.transpose(jnp.broadcast_to(row, (T, T)))

    def forward(i):
        p = (c + 1 + i) % nctx
        s = dot_nt(qh[at(p * T, T), :], kh[...]) * scale
        same = segcol[at(p * T, T), 0:1] == segrow[0:1, :].astype(F32)
        s = jnp.where(same, s, MASKED)
        e = jnp.exp(s - jnp.max(s, axis=1, keepdims=True))
        probs = (e / jnp.sum(e, axis=1, keepdims=True)).astype(BF16)
        attsend[at(p * T, T), :] = dot_nn(probs, vh[...]).astype(BF16)

        @pl.when(i < nctx - 1)
        def _():
            rcopy(attsend.at[at(p * T, T)], att.at[:, at(c * HD, HD)], att_ss.at[p], att_rs.at[c], {"ctx": p}).start()

    loop(0, nctx, forward)
    att[:, at(c * HD, HD)] = attsend[at(c * T, T), :]

    def ag_rows(owner, g):
        return at(owner * BR + g * RG, RG, 16)

    def gather_send(w, buf, phase):
        for g in range(GROUPS):
            lang_wait(phase, max(1, g * LG), (g + 1) * LG)
            rows = at(c * BR + g * RG, RG, 16)
            for j in range(J):
                buf[rows, j * HD : (j + 1) * HD] = dot_nn(
                    spread[j * RG : (j + 1) * RG, :], msg_r[phase, g * LG * MR : (g + 1) * LG * MR, :]
                ).astype(BF16)
            n = w * GROUPS + g
            rcopy(buf.at[rows], buf.at[rows], ag_ss.at[n, x], ag_rs.at[n, c], {"ctx": sib}).start()

            def one(i):
                xt = (x + i) % X
                rcopy(buf.at[rows], buf.at[rows], ag_ss.at[n, xt], ag_rs.at[n, c], {"ctx": xt * 2 + core}).start()

            loop(1, X, one)

    def gather_wait(w, buf, owner):
        for g in range(GROUPS):
            rows = ag_rows(owner, g)
            n = w * GROUPS + g
            rcopy(buf.at[rows], buf.at[rows], ag_fs.at[n, owner // 2], ag_rs.at[n, owner], {"ctx": sib}).wait_recv()

    def gather_forward(w, buf, xt):
        owner = xt * 2 + core
        for g in range(GROUPS):
            rows = ag_rows(owner, g)
            n = w * GROUPS + g
            copy = rcopy(buf.at[rows], buf.at[rows], ag_fs.at[n, xt], ag_rs.at[n, owner], {"ctx": sib})
            copy.wait_recv()
            copy.start()

    gather_send(0, rows_g, 0)

    def wait_att(i):
        p = (c + i) % nctx
        rcopy(attsend.at[at(p * T, T)], att.at[:, at(p * HD, HD)], att_ss.at[p], att_rs.at[p], {"ctx": p}).wait_recv()

    loop(1, nctx, wait_att)
    summed = residual[...].astype(F32) + att[...].astype(F32)
    summed_s[...] = summed
    inv_rms = lax.rsqrt(jnp.mean(summed * summed, axis=1, keepdims=True) + EPSILON)
    normed = summed * inv_rms
    normed_s[...] = normed
    dispatch(1, (normed * gain[...]).astype(BF16))

    for j in range(J):
        hit = lax.broadcasted_iota(jnp.int32, (T, nlang * MR), 1) == slot_col + PITCH * j
        sel_t[j * T : (j + 1) * T, :] = jnp.where(hit, 1.0, 0.0).astype(BF16)
    o_row = lax.broadcasted_iota(jnp.int32, (LG * MR, OP), 1)
    base_row = ((o_row * 205) >> 10) * (MR - CAP) + o_row
    inside = o_row < RG
    for j in range(J):
        hit = (lax.broadcasted_iota(jnp.int32, (LG * MR, OP), 0) == base_row + PITCH * j) & inside
        spread_t[:, j * OP : (j + 1) * OP] = jnp.where(hit, 1.0, 0.0).astype(BF16)
    stack_r[...] = jnp.zeros_like(stack_r)

    def turn(i):
        return (x + i + i // 2 - 2 * (i // 3)) % X

    loop(1, X, lambda i: gather_forward(0, rows_g, turn(i)))

    def back_probs(p):
        s = dot_nt(kh[...], qh[at(p * T, T), :]) * scale
        same = segcol[...] == segrow[0:1, at(p * T, T)].astype(F32)
        s = jnp.where(same, s, MASKED)
        e = jnp.exp(s - jnp.max(s, axis=0, keepdims=True))
        probs_t[at(p * L, L), :] = e / jnp.sum(e, axis=0, keepdims=True)

    loop(0, nctx, back_probs)
    weight_in[0].wait()
    PB = 2 * BR

    def grad_hidden(i):
        xt = turn(i)
        gather_wait(0, rows_g, xt * 2 + 1 - core)
        gh_s[at(xt * PB, PB), :] = dot_nt(rows_g[at(xt * PB, PB), :], wd[...])

    loop(0, X, grad_hidden)
    weight_in[1].wait()
    weight_in[2].wait()

    gather_send(1, rows_n, 1)
    FT = min(F, 256)
    DT = min(D, 512)

    def pair_copy(w, xt):
        return rcopy(
            part.at[w, at(xt * PB + (1 - core) * BR, BR, 16)],
            pair_r.at[w, at(xt * BR, BR, 16)],
            pair_ss.at[w, xt],
            pair_rs.at[w, xt],
            {"ctx": sib},
        )

    def pair_sum(w, xt):
        pair_copy(w, xt).wait_recv()
        own = part[w, at(xt * PB + core * BR, BR, 16), :].astype(F32)
        sum_s[w, at(xt * BR, BR, 16), :] = (own + pair_r[w, at(xt * BR, BR, 16), :].astype(F32)).astype(BF16)

    def fin_copy(w, xt, sender):
        return rcopy(
            sum_s.at[w, at(xt * BR, BR, 16)],
            fin_r.at[w, at(sender * BR, BR, 16)],
            fin_ss.at[w, xt],
            fin_rs.at[w, sender],
            {"ctx": xt * 2 + core},
        )

    def feed(i):
        xt = turn(i)
        rows = at(xt * PB, PB, 16)
        gather_wait(1, rows_n, xt * 2 + 1 - core)
        for n in range(F // FT):
            cols = slice(n * FT, (n + 1) * FT)
            block = rows_n[rows, :]
            pre_gate = dot_nn(block, wg[:, cols])
            pre_up = dot_nn(block, wu[:, cols])
            gh = gh_s[rows, cols]
            sig = jax.nn.sigmoid(pre_gate)
            silu = pre_gate * sig
            hid_s[rows, cols] = (silu * pre_up).astype(BF16)
            ggp_s[rows, cols] = (gh * pre_up * sig * (1.0 + pre_gate * (1.0 - sig))).astype(BF16)
            gup_s[rows, cols] = (gh * silu).astype(BF16)

        @pl.when(i < X - 1)
        def _():
            gather_forward(1, rows_n, turn(i + 1))

        for n in range(D // DT):
            cols = slice(n * DT, (n + 1) * DT)
            part[0, rows, cols] = (dot_nt(ggp_s[rows, :], wg[cols, :]) + dot_nt(gup_s[rows, :], wu[cols, :])).astype(BF16)
        pair_copy(0, xt).start()

        @pl.when(i > 0)
        def _():
            pair_sum(0, turn(i - 1))

        @pl.when(i > 1)
        def _():
            fin_copy(0, turn(i - 1), x).start()

    loop(0, X, feed)
    pair_sum(0, turn(X - 1))
    fin_copy(0, turn(X - 1), x).start()

    def down(i):
        xt = turn(i)
        rows = at(xt * PB, PB, 16)
        part[1, rows, :] = dot_nn(hid_s[rows, :], wd[...]).astype(BF16)
        pair_copy(1, xt).start()

    loop(0, X, down)

    def grad_w(n):
        cols = at(n * FT, FT)
        turned = jnp.transpose(rows_n[:, cols])
        gwg[cols, :] = dot_nn(turned, ggp_s[...]).astype(BF16)
        gwu[cols, :] = dot_nn(turned, gup_s[...]).astype(BF16)

    def grad_wd(n):
        cols = at(n * FT, FT)
        gwd[cols, :] = dot_nn(jnp.transpose(hid_s[:, cols]), rows_g[...]).astype(BF16)

    half = max(1, (D // FT) // 2)
    loop(0, half, grad_w)

    def return_send(w, phase):
        loop(1, X, lambda i: fin_copy(w, turn(i), turn(i)).wait_recv())
        for g in range(GROUPS):
            total = sum_s[w, at(x * BR + g * RG, RG, 16), :].astype(F32)
            for i in range(1, X):
                total = total + fin_r[w, at((x + i) % X * BR + g * RG, RG, 16), :].astype(F32)
            total = total.astype(BF16)
            for j in range(J):
                stack_r[j * OP : j * OP + RG, :] = total[:, j * HD : (j + 1) * HD]
            msg_s[phase, g * LG * MR : (g + 1) * LG * MR, :] = dot_nn(spread_t[...], stack_r[...]).astype(BF16)

            def one(d):
                to = (me + nlang - d) % nlang
                rcopy(
                    msg_s.at[phase, at(d * MR, MR)],
                    msg_r.at[phase, at(me * MR, MR)],
                    lang_ss.at[phase, d],
                    lang_rs.at[phase, me],
                    {"lang": to},
                ).start()

            loop(max(1, g * LG), (g + 1) * LG, one)
        msg_r[phase, at(me * MR, MR), :] = msg_s[phase, 0:MR, :]

    def combine(phase):
        lang_wait_but_own(phase)
        for j in range(J):
            gn_s[:, j * HD : (j + 1) * HD] = dot_nn(sel_t[j * T : (j + 1) * T, :], msg_r[phase])

    return_send(0, 2)

    def down_sum(i):
        pair_sum(1, turn(i))

        @pl.when(i > 0)
        def _():
            fin_copy(1, turn(i), x).start()

    loop(0, X, down_sum)
    loop(half, D // FT, grad_w)
    out_w = [
        pltpu.make_async_copy(src, dst, out_sem.at[i])
        for i, (src, dst) in enumerate(((gwg, gwg_hbm), (gwu, gwu_hbm), (gwd, gwd_hbm)))
    ]
    out_w[0].start()
    out_w[1].start()
    loop(0, F // FT, grad_wd)
    out_w[2].start()

    combine(2)
    grad_normin = gn_s[...]
    normed = normed_s[...]
    summed = summed_s[...]
    inv_rms = lax.rsqrt(jnp.mean(summed * summed, axis=1, keepdims=True) + EPSILON)
    scaled = grad_normin * gain[...]
    gres = gout_s[...] + inv_rms * (scaled - normed * jnp.mean(scaled * normed, axis=1, keepdims=True))
    grsend[...] = gres.astype(BF16)

    def gr_copy(to, owner, sem_at):
        return rcopy(grsend.at[:, at(to * HD, HD)], grh.at[at(owner * T, T)], gr_ss.at[sem_at], gr_rs.at[owner], {"ctx": to})

    loop(1, nctx, lambda i: gr_copy((c + i) % nctx, c, (c + i) % nctx).start())
    grh[at(c * T, T), :] = grsend[:, at(c * HD, HD)]
    grad_res[...] = grsend[...]
    gain_part = jnp.sum(grad_normin * normed, axis=0, keepdims=True)
    for j in range(J):
        gain_s[j : j + 1, :] = gain_part[:, j * HD : (j + 1) * HD]

    def gain_copy(to, owner):
        return rcopy(gain_s, gain_c.at[owner], gain_ss.at[to], gain_rs.at[owner], {"ctx": to})

    loop(1, nctx, lambda i: gain_copy((c + i) % nctx, c).start())
    gain_c[c] = gain_s[...]

    return_send(1, 3)

    gk_acc[...] = jnp.zeros_like(gk_acc)
    gv_acc[...] = jnp.zeros_like(gv_acc)

    def go_copy(n, src, dst, to, owner):
        return rcopy(src.at[at(to * T, T)], dst.at[:, at(owner * HD, HD)], go_ss.at[n, to], go_rs.at[n, owner], {"ctx": to})

    def backward(i):
        p = (c + i) % nctx

        @pl.when(i > 0)
        def _():
            gr_copy(p, p, p).wait_recv()

        gr = grh[at(p * T, T), :]
        probs = probs_t[at(p * L, L), :]
        gp = dot_nt(vh[...], gr)
        gs = (probs * (gp - jnp.sum(probs * gp, axis=0, keepdims=True))).astype(BF16)
        gqsend[at(p * T, T), :] = (dot_nn(jnp.transpose(gs), kh[...]) * scale).astype(BF16)

        @pl.when(i > 0)
        def _():
            go_copy(0, gqsend, gq_hbm, p, c).start()

        gv_acc[...] += dot_nn(probs.astype(BF16), gr)
        gk_acc[...] += dot_nn(gs, qh[at(p * T, T), :])

    loop(0, nctx, backward)
    gksend[...] = (gk_acc[...] * scale).astype(BF16)
    gvsend[...] = gv_acc[...].astype(BF16)

    def send_kv(i):
        p = (c + i) % nctx
        go_copy(1, gksend, gk_hbm, p, c).start()
        go_copy(2, gvsend, gv_hbm, p, c).start()

    loop(1, nctx, send_kv)
    triples = ((gqsend, gq_hbm), (gksend, gk_hbm), (gvsend, gv_hbm))
    own_out = [
        pltpu.make_async_copy(src.at[at(c * T, T)], dst.at[:, at(c * HD, HD)], loc_sem.at[3 + n])
        for n, (src, dst) in enumerate(triples)
    ]
    for copy in own_out:
        copy.start()

    loop(1, nctx, lambda i: gain_copy((c + i) % nctx, (c + i) % nctx).wait_recv())
    gain_l_s[...] = jnp.sum(gain_c[...], axis=0)

    def gainl_copy(to, owner):
        return rcopy(gain_l_s, gain_l.at[owner], gainl_ss.at[to], gainl_rs.at[owner], {"lang": to})

    loop(1, nlang, lambda i: gainl_copy((me + i) % nlang, me).start())
    gain_l[me] = gain_l_s[...]

    combine(3)
    layer_out[...] = (summed_s[...] + gn_s[...]).astype(BF16)

    loop(1, nlang, lambda i: gainl_copy((me + i) % nlang, (me + i) % nlang).wait_recv())
    grad_gain[...] = jnp.sum(gain_l[...], axis=0)

    def wait_out(i):
        p = (c + i) % nctx
        for n, (src, dst) in enumerate(triples):
            go_copy(n, src, dst, p, p).wait_recv()

    loop(1, nctx, wait_out)

    def sent_ctx(i):
        p = (c + i) % nctx
        for copy in in_copies(p, c, p):
            copy.wait_send()
        rcopy(attsend.at[at(p * T, T)], att.at[:, at(c * HD, HD)], att_ss.at[p], att_rs.at[c], {"ctx": p}).wait_send()
        gr_copy(p, c, p).wait_send()
        gain_copy(p, c).wait_send()
        for n, (src, dst) in enumerate(triples):
            go_copy(n, src, dst, p, c).wait_send()

    loop(1, nctx, sent_ctx)

    def sent_lang(d):
        for phase in range(4):
            rcopy(
                msg_s.at[phase, at(d * MR, MR)],
                msg_r.at[phase, at(d * MR, MR)],
                lang_ss.at[phase, d],
                lang_rs.at[phase, d],
                {"lang": (me + d) % nlang},
            ).wait_send()
        gainl_copy((me + d) % nlang, me).wait_send()

    loop(1, nlang, sent_lang)

    def sent_gather(i):
        xt = (x + i) % X
        for w, buf in ((0, rows_g), (1, rows_n)):
            for g in range(GROUPS):
                n = w * GROUPS + g
                rows = ag_rows(c, g)
                rcopy(buf.at[rows], buf.at[rows], ag_ss.at[n, xt], ag_rs.at[n, c], {"ctx": sib}).wait_send()

                @pl.when(i > 0)
                def _():
                    far = ag_rows(xt * 2 + core, g)
                    rcopy(buf.at[far], buf.at[far], ag_fs.at[n, xt], ag_rs.at[n, c], {"ctx": sib}).wait_send()

            pair_copy(w, xt).wait_send()

            @pl.when(i > 0)
            def _():
                fin_copy(w, xt, x).wait_send()

    loop(0, X, sent_gather)
    for copy in own_out:
        copy.wait()
    for copy in out_w:
        copy.wait()


def local(
    attn_queries,
    attn_keys,
    attn_values,
    residual,
    cotangent,
    segment_ids,
    language_ids,
    token_counts,
    norm_gain,
    gate_weight,
    up_weight,
    down_weight,
):
    nctx = lax.axis_size("ctx")
    nlang = lax.axis_size("lang")
    T, D = attn_queries.shape[1:]
    F = gate_weight.shape[2]
    L = nctx * T
    J = D // HD
    X = nctx // 2
    MR = PITCH * J
    LG = nlang // GROUPS
    RG = LG * CAP
    BR = nlang * CAP
    R = nctx * BR
    vmem = lambda *shape: pltpu.VMEM(shape, BF16)
    vmem32 = lambda *shape: pltpu.VMEM(shape, F32)
    dma = lambda *shape: pltpu.SemaphoreType.DMA(shape)
    scratch = [
        vmem(L, HD),
        vmem(L, HD),
        vmem(L, HD),
        vmem(16, T),
        vmem(16, L),
        vmem32(L, T),
        vmem32(nctx * L, T),
        vmem(L, HD),
        vmem(T, D),
        vmem(D, F),
        vmem(D, F),
        vmem(F, D),
        vmem(D, F),
        vmem(D, F),
        vmem(F, D),
        vmem32(T, D),
        vmem32(T, D),
        vmem32(T, D),
        vmem32(T, D),
        vmem(J * T, HD),
        vmem(nlang * MR, J * T),
        vmem(J * T, nlang * MR),
        vmem(J * RG, LG * MR),
        vmem(LG * MR, J * 128),
        vmem(J * 128, HD),
        vmem(4, nlang * MR, HD),
        vmem(4, nlang * MR, HD),
        vmem(R, D),
        vmem(R, D),
        vmem32(R, F),
        vmem(R, F),
        vmem(R, F),
        vmem(R, F),
        vmem(2, R, D),
        vmem(2, X * BR, D),
        vmem(2, X * BR, D),
        vmem(2, X * BR, D),
        vmem(T, D),
        vmem(L, HD),
        vmem(L, HD),
        vmem32(L, HD),
        vmem32(L, HD),
        vmem(L, HD),
        vmem(L, HD),
        vmem32(J, HD),
        vmem32(nctx, J, HD),
        vmem32(J, HD),
        vmem32(nlang, J, HD),
        dma(6),
        dma(3),
        dma(4, nctx),
        dma(4, nctx),
        dma(nctx),
        dma(nctx),
        dma(4, nlang),
        dma(4, nlang),
        dma(2 * GROUPS, X),
        dma(2 * GROUPS, X),
        dma(2 * GROUPS, nctx),
        dma(2, X),
        dma(2, X),
        dma(2, X),
        dma(2, X),
        dma(nctx),
        dma(nctx),
        dma(3, nctx),
        dma(3, nctx),
        dma(nctx),
        dma(nctx),
        dma(nlang),
        dma(nlang),
    ]
    anywhere = pl.BlockSpec(memory_space=pl.ANY)
    inside = pl.BlockSpec(memory_space=pltpu.VMEM)
    shape = lambda *dims: jax.ShapeDtypeStruct(dims, BF16)
    outs = pl.pallas_call(
        functools.partial(kernel, nctx, nlang),
        out_shape=(
            shape(T, D),
            shape(T, D),
            shape(T, D),
            shape(T, D),
            shape(T, D),
            jax.ShapeDtypeStruct((J, HD), F32),
            shape(D, F),
            shape(D, F),
            shape(F, D),
        ),
        in_specs=[anywhere] * 3 + [inside] * 6 + [anywhere] * 3,
        out_specs=(inside, anywhere, anywhere, anywhere, inside, inside, anywhere, anywhere, anywhere),
        scratch_shapes=scratch,
        compiler_params=pltpu.CompilerParams(collective_id=0, has_side_effects=True, vmem_limit_bytes=58 * 1024 * 1024),
        cost_estimate=pl.CostEstimate(flops=16_000_000_000, bytes_accessed=10_000_000, transcendentals=3_000_000),
        name="layer",
    )(
        attn_queries[0],
        attn_keys[0],
        attn_values[0],
        residual[0],
        cotangent[0],
        segment_ids,
        language_ids.reshape(1, T),
        token_counts.reshape(1, nlang),
        norm_gain.reshape(1, D),
        gate_weight[0],
        up_weight[0],
        down_weight[0],
    )
    layer_out, gq, gk, gv, gres, ggain, gwg, gwu, gwd = outs
    return (
        layer_out[None],
        gq[None],
        gk[None],
        gv[None],
        gres[None],
        ggain.reshape(D),
        gwg[None],
        gwu[None],
        gwd[None],
    )


def solution(mesh):
    block = P("lang", "ctx", None)
    in_specs = (
        block,
        block,
        block,
        block,
        block,
        P("lang", "ctx"),
        block,
        P(),
        P(),
        P("lang", None, "ctx"),
        P("lang", None, "ctx"),
        block,
    )
    out_specs = (
        block,
        block,
        block,
        block,
        block,
        P(),
        P("lang", None, "ctx"),
        P("lang", None, "ctx"),
        block,
    )
    return jax.shard_map(local, mesh=mesh, in_specs=in_specs, out_specs=out_specs, check_vma=False)
```

```python
import functools

import jax
import jax.numpy as jnp
from jax import lax
from jax.experimental import pallas as pl
from jax.experimental.pallas import tpu as pltpu
from jax.sharding import PartitionSpec as P

HD = 128
EPSILON = 1e-06
CAP = 5
PITCH = 6
GROUPS = 2
MESH = pl.DeviceIdType.MESH
F32 = jnp.float32
BF16 = jnp.bfloat16
MASKED = -1e30


def dot_nn(a, b):
    return lax.dot_general(a, b, (((1,), (0,)), ((), ())), preferred_element_type=F32)


def dot_nt(a, b):
    return lax.dot_general(a, b, (((1,), (1,)), ((), ())), preferred_element_type=F32)


def at(start, size, step=None):
    return pl.ds(pl.multiple_of(start, step or size), size)


def kernel(
    nctx,
    nlang,
    q_hbm,
    k_hbm,
    v_hbm,
    residual,
    cotangent,
    segment,
    language,
    counts,
    gain,
    wg_hbm,
    wu_hbm,
    wd_hbm,
    layer_out,
    gq_hbm,
    gk_hbm,
    gv_hbm,
    grad_res,
    grad_gain,
    gwg_hbm,
    gwu_hbm,
    gwd_hbm,
    qh,
    kh,
    vh,
    segsend,
    segrow,
    segcol,
    probs_t,
    probs_h,
    attsend,
    att,
    wg,
    wu,
    wd,
    gwg,
    gwu,
    gwd,
    summed_s,
    normed_s,
    gout_s,
    gn_s,
    stack,
    sel,
    sel_t,
    spread,
    spread_t,
    stack_r,
    msg_s,
    msg_r,
    rows_n,
    rows_g,
    gh_s,
    hid_s,
    ggp_s,
    gup_s,
    part,
    pair_r,
    sum_s,
    mid_r,
    fin_r,
    grsend,
    grh,
    gqsend,
    gksend,
    gvsend,
    gain_s,
    gain_c,
    gain_l_s,
    gain_l,
    loc_sem,
    out_sem,
    in_s,
    in_r,
    att_ss,
    att_rs,
    lang_ss,
    lang_rs,
    near_ss,
    near_rs,
    half_ss,
    half_rs,
    sib_ss,
    sib_rs,
    pair_ss,
    pair_rs,
    mid_ss,
    mid_rs,
    fin_ss,
    fin_rs,
    gr_ss,
    gr_rs,
    go_ss,
    go_rs,
    gain_ss,
    gain_rs,
    gainl_ss,
    gainl_rs,
):
    T, D = residual.shape
    L = nctx * T
    J = D // HD
    X = nctx // 2
    assert X == 4
    F = wg.shape[1]
    H = D // 2
    MR = PITCH * J
    LG = nlang // GROUPS
    RG = LG * CAP
    OP = 128
    scale = HD ** (-0.5)
    c = lax.axis_index("ctx")
    me = lax.axis_index("lang")
    x = c // 2
    core = c % 2
    sib = x * 2 + 1 - core
    right, left, across = (x + 1) % X, (x + 3) % X, (x + 2) % X

    def rcopy(src, dst, ssem, rsem, dev):
        return pltpu.make_async_remote_copy(
            src_ref=src, dst_ref=dst, send_sem=ssem, recv_sem=rsem, device_id=dev, device_id_type=MESH
        )

    def loop(lo, hi, body):
        def step(i, carry):
            body(i)
            return carry

        lax.fori_loop(lo, hi, step, 0)

    scope = []

    def mark(name):
        if scope:
            scope.pop().__exit__(None, None, None)
        if name:
            scope.append(jax.named_scope(name))
            scope[-1].__enter__()

    mark("entry")
    weight_in = [
        pltpu.make_async_copy(src, dst, loc_sem.at[i])
        for i, (src, dst) in enumerate(((wd_hbm, wd), (wg_hbm, wg), (wu_hbm, wu)))
    ]
    own_in = [
        pltpu.make_async_copy(src.at[:, at(c * HD, HD)], dst.at[at(c * T, T)], loc_sem.at[3 + i])
        for i, (src, dst) in enumerate(((k_hbm, kh), (q_hbm, qh), (v_hbm, vh)))
    ]
    segsend[...] = jnp.broadcast_to(segment[...].astype(F32), segsend.shape).astype(BF16)

    barrier = pltpu.get_barrier_semaphore()
    loop(1, nctx, lambda i: pl.semaphore_signal(barrier, inc=1, device_id={"ctx": (c + i) % nctx}, device_id_type=MESH))
    loop(1, nlang, lambda i: pl.semaphore_signal(barrier, inc=1, device_id={"lang": (me + i) % nlang}, device_id_type=MESH))
    for copy in own_in:
        copy.start()
    pl.semaphore_wait(barrier, nctx - 1 + nlang - 1)

    mark("send_qkv")
    def in_copy(i, to, owner):
        if i == 3:
            src, dst = segsend, segrow.at[:, at(owner * T, T)]
        else:
            src, dst = ((k_hbm, kh), (q_hbm, qh), (v_hbm, vh))[i]
            src, dst = src.at[:, at(to * HD, HD)], dst.at[at(owner * T, T)]
        return rcopy(src, dst, in_s.at[i, to], in_r.at[i, owner], {"ctx": to})

    for which in ((3, 0), (1,), (2,)):

        def send_in(i):
            for n in which:
                in_copy(n, (c + i) % nctx, c).start()

        loop(1, nctx, send_in)
    for copy in weight_in:
        copy.start()
    segrow[:, at(c * T, T)] = segsend[...]

    mark("slots")
    lang_row = language[...].astype(F32)
    lang_col = jnp.transpose(jnp.broadcast_to(lang_row, (T, T)))
    earlier = lax.broadcasted_iota(jnp.int32, (T, T), 0) < lax.broadcasted_iota(jnp.int32, (T, T), 1)
    rank = jnp.sum(jnp.where((lang_col == lang_row) & earlier, 1.0, 0.0), axis=0, keepdims=True)
    slot_row = lang_row * float(MR) + rank
    slot_col = jnp.transpose(jnp.broadcast_to(slot_row, (T, T)))[:, 0:1].astype(jnp.int32)
    slot_row = slot_row.astype(jnp.int32)
    for j in range(J):
        hit = lax.broadcasted_iota(jnp.int32, (nlang * MR, T), 0) == slot_row + PITCH * j
        sel[:, j * T : (j + 1) * T] = jnp.where(hit, 1.0, 0.0).astype(BF16)

    lang_hit = lang_col[:, 0:1] == lax.broadcasted_iota(jnp.int32, (T, nlang), 1).astype(F32)
    count = jnp.sum(jnp.where(lang_hit, counts[...].astype(F32), 0.0), axis=1, keepdims=True)
    gout_s[...] = cotangent[...].astype(F32) * (16.0 * lax.rsqrt(count))

    NY = 4 if nlang % 8 == 0 else 1
    NZ = nlang // NY

    def partner(d, sign):
        if NY == 1:
            return (me + nlang + sign * d) % nlang
        turn_z = d // NY
        off_z = (2 * turn_z) % NZ + turn_z // (NZ // 2)
        return (me // NY + NZ + sign * off_z) % NZ * NY + (me % NY + NY + sign * (d % NY)) % NY

    def dispatch(phase, stacked):
        for j in range(J):
            stack[j * T : (j + 1) * T, :] = stacked[:, j * HD : (j + 1) * HD]
        msg_s[phase] = dot_nn(sel[...], stack[...]).astype(BF16)

        def one(d):
            to = partner(d, 1)
            rcopy(
                msg_s.at[phase, at(to * MR, MR)],
                msg_r.at[phase, at(d * MR, MR)],
                lang_ss.at[phase, d],
                lang_rs.at[phase, d],
                {"lang": to},
            ).start()

        loop(1, nlang, one)
        msg_r[phase, 0:MR, :] = msg_s[phase, at(me * MR, MR), :]

    def lang_wait(phase, lo, hi):
        def one(d):
            rcopy(
                msg_s.at[phase, at(d * MR, MR)],
                msg_r.at[phase, at(d * MR, MR)],
                lang_ss.at[phase, d],
                lang_rs.at[phase, d],
                {"lang": me},
            ).wait_recv()

        loop(lo, hi, one)

    def lang_wait_but_own(phase):
        def one(d):
            l = (me + d) % nlang
            rcopy(
                msg_s.at[phase, at(l * MR, MR)],
                msg_r.at[phase, at(l * MR, MR)],
                lang_ss.at[phase, d],
                lang_rs.at[phase, l],
                {"lang": me},
            ).wait_recv()

        loop(1, nlang, one)

    mark("dispatch_grads")
    dispatch(0, gout_s[...].astype(BF16))

    mark("spread")
    o_col = lax.broadcasted_iota(jnp.int32, (RG, LG * MR), 0)
    base = ((o_col * 205) >> 10) * (MR - CAP) + o_col
    for j in range(J):
        hit = lax.broadcasted_iota(jnp.int32, (RG, LG * MR), 1) == base + PITCH * j
        spread[j * RG : (j + 1) * RG, :] = jnp.where(hit, 1.0, 0.0).astype(BF16)

    mark("wait_qkv")
    for copy in own_in:
        copy.wait()

    def wait_in(n):
        loop(1, nctx, lambda i: in_copy(n, (c + i) % nctx, (c + i) % nctx).wait_recv())

    for n in (3, 0, 1):
        wait_in(n)
    for p in range(nctx):
        row = segrow[0:1, p * T : (p + 1) * T].astype(F32)
        segcol[p * T : (p + 1) * T, :] = jnp.transpose(jnp.broadcast_to(row, (T, T)))

    mark("attention")
    def forward(i):
        p = (c + 1 + i) % nctx
        s = dot_nt(qh[at(p * T, T), :], kh[...]) * scale
        same = segcol[at(p * T, T), 0:1] == segrow[0:1, :].astype(F32)
        s = jnp.where(same, s, MASKED)
        e = jnp.exp(s - jnp.max(s, axis=1, keepdims=True))
        probs_h[at(i * T, T), :] = (e / jnp.sum(e, axis=1, keepdims=True)).astype(BF16)

    loop(0, nctx, forward)
    mark("wait_values")
    wait_in(2)
    mark("attended")

    def attend(i):
        p = (c + 1 + i) % nctx
        attsend[at(p * T, T), :] = dot_nn(probs_h[at(i * T, T), :], vh[...]).astype(BF16)

        @pl.when(i < nctx - 1)
        def _():
            rcopy(attsend.at[at(p * T, T)], att.at[:, at(c * HD, HD)], att_ss.at[p], att_rs.at[c], {"ctx": p}).start()

    loop(0, nctx, attend)
    att[:, at(c * HD, HD)] = attsend[at(c * T, T), :]

    def block(chip, g, k):
        return at(((chip * GROUPS + g) * 2 + k) * RG, RG, 16)

    def near_copy(w, buf, g, side):
        rows = block(x, g, core)
        to = (right, left)[side] * 2 + core
        n = w * GROUPS + g
        return rcopy(buf.at[rows], buf.at[rows], near_ss.at[n, side], near_rs.at[n, side], {"ctx": to})

    def half_copy(w, buf, g, side):
        rows = block((left, right)[side], g, core)
        cols = slice(side * H, (side + 1) * H)
        to = (right, left)[side] * 2 + core
        n = w * GROUPS + g
        return rcopy(buf.at[rows, cols], buf.at[rows, cols], half_ss.at[n, side], half_rs.at[n, side], {"ctx": to})

    def sib_copy(w, buf, g, what, k=core):
        n = w * GROUPS + g
        rows = block((x, left, right, across, across)[what], g, k)
        cols = slice(None) if what < 3 else slice((what - 3) * H, (what - 2) * H)
        return rcopy(buf.at[rows, cols], buf.at[rows, cols], sib_ss.at[n, what], sib_rs.at[n, what], {"ctx": sib})

    def gather_send(w, buf, phase, g):
        lang_wait(phase, max(1, g * LG), (g + 1) * LG)
        rows = block(x, g, core)
        for j in range(J):
            buf[rows, j * HD : (j + 1) * HD] = dot_nn(
                spread[j * RG : (j + 1) * RG, :], msg_r[phase, g * LG * MR : (g + 1) * LG * MR, :]
            ).astype(BF16)
        near_copy(w, buf, g, 0).start()
        near_copy(w, buf, g, 1).start()
        sib_copy(w, buf, g, 0).start()

    def near_forward(w, buf, g):
        for side in range(2):
            rows = block((left, right)[side], g, core)
            n = w * GROUPS + g
            rcopy(buf.at[rows], buf.at[rows], near_ss.at[n, side], near_rs.at[n, side], {"ctx": sib}).wait_recv()
            half_copy(w, buf, g, side).start()
            sib_copy(w, buf, g, 1 + side).start()

    def half_forward(w, buf, g):
        for side in range(2):
            rows = block(across, g, core)
            cols = slice(side * H, (side + 1) * H)
            n = w * GROUPS + g
            rcopy(
                buf.at[rows, cols], buf.at[rows, cols], half_ss.at[n, side], half_rs.at[n, side], {"ctx": sib}
            ).wait_recv()
            sib_copy(w, buf, g, 3 + side).start()

    def sib_wait(w, buf, g, what):
        sib_copy(w, buf, g, what, 1 - core).wait_recv()

    mark("grad_rows")
    for g in range(GROUPS):
        gather_send(0, rows_g, 0, g)

    mark("wait_attended")
    def wait_att(i):
        p = (c + i) % nctx
        rcopy(attsend.at[at(p * T, T)], att.at[:, at(p * HD, HD)], att_ss.at[p], att_rs.at[p], {"ctx": p}).wait_recv()

    loop(1, nctx, wait_att)
    mark("norm_dispatch")
    summed = residual[...].astype(F32) + att[...].astype(F32)
    summed_s[...] = summed
    inv_rms = lax.rsqrt(jnp.mean(summed * summed, axis=1, keepdims=True) + EPSILON)
    normed = summed * inv_rms
    normed_s[...] = normed
    dispatch(1, (normed * gain[...]).astype(BF16))

    mark("layouts")
    for j in range(J):
        hit = lax.broadcasted_iota(jnp.int32, (T, nlang * MR), 1) == slot_col + PITCH * j
        sel_t[j * T : (j + 1) * T, :] = jnp.where(hit, 1.0, 0.0).astype(BF16)
    o_row = lax.broadcasted_iota(jnp.int32, (LG * MR, OP), 1)
    base_row = ((o_row * 205) >> 10) * (MR - CAP) + o_row
    inside = o_row < RG
    for j in range(J):
        hit = (lax.broadcasted_iota(jnp.int32, (LG * MR, OP), 0) == base_row + PITCH * j) & inside
        spread_t[:, j * OP : (j + 1) * OP] = jnp.where(hit, 1.0, 0.0).astype(BF16)
    stack_r[...] = jnp.zeros_like(stack_r)

    mark("back_probs")

    def back_probs(p):
        s = dot_nt(kh[...], qh[at(p * T, T), :]) * scale
        same = segcol[...] == segrow[0:1, at(p * T, T)].astype(F32)
        s = jnp.where(same, s, MASKED)
        e = jnp.exp(s - jnp.max(s, axis=0, keepdims=True))
        probs = e / jnp.sum(e, axis=0, keepdims=True)
        probs_t[at(p * L, L), :] = probs
        probs_h[:, at(p * T, T)] = probs.astype(BF16)

    loop(0, nctx, back_probs)
    mark("forward_grads")
    for g in range(GROUPS):
        near_forward(0, rows_g, g)
    mark("norm_rows")
    for g in range(GROUPS):
        gather_send(1, rows_n, 1, g)
        half_forward(0, rows_g, g)
    mark("grad_hidden")
    weight_in[0].wait()
    CR = GROUPS * 2 * RG
    for g in range(GROUPS):
        for what in range(5):
            sib_wait(0, rows_g, g, what)

    def grad_hidden(i):
        rows = at(i * CR, CR, 16)
        gh_s[rows, :] = dot_nt(rows_g[rows, :], wd[...])

    loop(0, X, grad_hidden)
    weight_in[1].wait()
    weight_in[2].wait()

    FT = min(F, 256)
    DT = min(D, 512)

    def flat(chip, g):
        return at((chip * GROUPS + g) * RG, RG, 16)

    def pair_copy(w, chip, g):
        n = chip * GROUPS + g
        return rcopy(
            part.at[w, block(chip, g, 1 - core)], pair_r.at[w, flat(chip, g)], pair_ss.at[w, n], pair_rs.at[w, n], {"ctx": sib}
        )

    def pair_sum(w, chip, g, cols):
        own = part[w, block(chip, g, core), cols].astype(F32)
        return own + pair_r[w, flat(chip, g), cols].astype(F32)

    halves = (slice(0, H), slice(H, D))

    def mid_copy(w, g, h):
        to = (right, left)[h] * 2 + core
        src = sum_s.at[w, flat(across, g), halves[h]]
        n = w * GROUPS + g
        return rcopy(src, mid_r.at[w, at(g * RG, RG, 16), halves[h]], mid_ss.at[n, h], mid_rs.at[n, h], {"ctx": to})

    def fin_copy(w, g, side, h):
        chip = (right, left)[side]
        src = sum_s.at[w, flat(chip, g), halves[h]]
        dst = fin_r.at[w, at((side * GROUPS + g) * RG, RG, 16), halves[h]]
        n = w * GROUPS + g
        return rcopy(src, dst, fin_ss.at[n, side * 2 + h], fin_rs.at[n, side * 2 + h], {"ctx": chip * 2 + core})

    def sum_across(w, g):
        pair_copy(w, across, g).wait_recv()
        for h in range(2):
            sum_s[w, flat(across, g), halves[h]] = pair_sum(w, across, g, halves[h]).astype(BF16)
            mid_copy(w, g, h).start()

    def sum_near(w, g, side):
        chip, h = (right, left)[side], 1 - side
        pair_copy(w, chip, g).wait_recv()
        sum_s[w, flat(chip, g), halves[h]] = pair_sum(w, chip, g, halves[h]).astype(BF16)
        fin_copy(w, g, side, h).start()

    def sum_late(w, g):
        for side in range(2):
            chip, h = (right, left)[side], side
            mid_copy(w, g, h).wait_recv()
            total = pair_sum(w, chip, g, halves[h]) + mid_r[w, at(g * RG, RG, 16), halves[h]].astype(F32)
            sum_s[w, flat(chip, g), halves[h]] = total.astype(BF16)
            fin_copy(w, g, side, h).start()

    def sum_own(w, g):
        pair_copy(w, x, g).wait_recv()
        for side in range(2):
            for h in range(2):
                fin_copy(w, g, side, h).wait_recv()
        total = pair_sum(w, x, g, slice(None))
        for side in range(2):
            total = total + fin_r[w, at((side * GROUPS + g) * RG, RG, 16), :].astype(F32)
        return total.astype(BF16)

    def feed(rows):
        for n in range(F // FT):
            cols = slice(n * FT, (n + 1) * FT)
            pre_gate = dot_nn(rows_n[rows, :], wg[:, cols])
            pre_up = dot_nn(rows_n[rows, :], wu[:, cols])
            gh = gh_s[rows, cols]
            sig = jax.nn.sigmoid(pre_gate)
            silu = pre_gate * sig
            hid_s[rows, cols] = (silu * pre_up).astype(BF16)
            ggp_s[rows, cols] = (gh * pre_up * sig * (1.0 + pre_gate * (1.0 - sig))).astype(BF16)
            gup_s[rows, cols] = (gh * silu).astype(BF16)
        for n in range(D // DT):
            cols = slice(n * DT, (n + 1) * DT)
            part[0, rows, cols] = (dot_nt(ggp_s[rows, :], wg[cols, :]) + dot_nt(gup_s[rows, :], wu[cols, :])).astype(BF16)

    def feed_chip(i):
        chip = (x + i + i // 2) % X
        for g in range(GROUPS):
            for what, when in ((0, 0), (2, 1), (1, 2)):

                @pl.when(i == when)
                def _():
                    sib_wait(1, rows_n, g, what)

        feed(at(chip * CR, CR, 16))
        for g in range(GROUPS):
            pair_copy(0, chip, g).start()

    mark("feed_own")
    loop(0, 1, feed_chip)
    mark("feed_near_wait")
    for g in range(GROUPS):
        near_forward(1, rows_n, g)
    mark("feed_near")
    loop(1, 3, feed_chip)
    mark("sum_near")
    for g in range(GROUPS):
        for side in range(2):
            sum_near(0, g, side)
    for g in range(GROUPS):
        half_forward(1, rows_n, g)
    mark("feed_across")

    def feed_across(g):
        for m in range(GROUPS):

            @pl.when(g == m)
            def _():
                sib_wait(1, rows_n, m, 3)
                sib_wait(1, rows_n, m, 4)

        feed(at((across * GROUPS + g) * 2 * RG, 2 * RG, 16))
        pair_copy(0, across, g).start()

    loop(0, GROUPS, feed_across)
    mark("sum_across")
    for g in range(GROUPS):
        sum_across(0, g)

    mark("down")

    def down(i):
        rows = at(i * CR, CR, 16)
        part[1, rows, :] = dot_nn(hid_s[rows, :], wd[...]).astype(BF16)
        for g in range(GROUPS):
            pair_copy(1, i, g).start()

    loop(0, X, down)
    mark("sum_late")
    for g in range(GROUPS):
        sum_late(0, g)

    def grad_w(n):
        cols = at(n * FT, FT)
        turned = jnp.transpose(rows_n[:, cols])
        gwg[cols, :] = dot_nn(turned, ggp_s[...]).astype(BF16)
        gwu[cols, :] = dot_nn(turned, gup_s[...]).astype(BF16)

    def grad_wd(n):
        cols = at(n * FT, FT)
        gwd[cols, :] = dot_nn(jnp.transpose(hid_s[:, cols]), rows_g[...]).astype(BF16)

    def return_send(w, phase):
        for g in range(GROUPS):
            total = sum_own(w, g)
            for j in range(J):
                stack_r[j * OP : j * OP + RG, :] = total[:, j * HD : (j + 1) * HD]
            msg_s[phase, g * LG * MR : (g + 1) * LG * MR, :] = dot_nn(spread_t[...], stack_r[...]).astype(BF16)

            def one(d):
                to = partner(d, -1)
                rcopy(
                    msg_s.at[phase, at(d * MR, MR)],
                    msg_r.at[phase, at(me * MR, MR)],
                    lang_ss.at[phase, d],
                    lang_rs.at[phase, me],
                    {"lang": to},
                ).start()

            loop(max(1, g * LG), (g + 1) * LG, one)
        msg_r[phase, at(me * MR, MR), :] = msg_s[phase, 0:MR, :]

    def combine(phase):
        lang_wait_but_own(phase)
        for j in range(J):
            gn_s[:, j * HD : (j + 1) * HD] = dot_nn(sel_t[j * T : (j + 1) * T, :], msg_r[phase])

    mark("grad_w_a")
    half = max(1, (D // FT) // 2)
    loop(0, half, grad_w)
    mark("return_grads")
    return_send(0, 2)
    mark("ffn_sums")
    for g in range(GROUPS):
        sum_across(1, g)
    for g in range(GROUPS):
        for side in range(2):
            sum_near(1, g, side)
    mark("grad_w_b")
    loop(half, D // FT, grad_w)
    mark("ffn_late")
    for g in range(GROUPS):
        sum_late(1, g)
    mark("grad_wd")
    out_w = [
        pltpu.make_async_copy(src, dst, out_sem.at[i])
        for i, (src, dst) in enumerate(((gwg, gwg_hbm), (gwu, gwu_hbm), (gwd, gwd_hbm)))
    ]
    out_w[0].start()
    out_w[1].start()
    loop(0, F // FT, grad_wd)
    out_w[2].start()

    mark("combine_grads")
    combine(2)
    mark("grad_residual")
    grad_normin = gn_s[...]
    normed = normed_s[...]
    summed = summed_s[...]
    inv_rms = lax.rsqrt(jnp.mean(summed * summed, axis=1, keepdims=True) + EPSILON)
    scaled = grad_normin * gain[...]
    gres = gout_s[...] + inv_rms * (scaled - normed * jnp.mean(scaled * normed, axis=1, keepdims=True))
    grsend[...] = gres.astype(BF16)

    def gr_copy(to, owner, sem_at):
        return rcopy(grsend.at[:, at(to * HD, HD)], grh.at[at(owner * T, T)], gr_ss.at[sem_at], gr_rs.at[owner], {"ctx": to})

    loop(1, nctx, lambda i: gr_copy((c + i) % nctx, c, (c + i) % nctx).start())
    grh[at(c * T, T), :] = grsend[:, at(c * HD, HD)]
    grad_res[...] = grsend[...]
    gain_part = jnp.sum(grad_normin * normed, axis=0, keepdims=True)
    for j in range(J):
        gain_s[j : j + 1, :] = gain_part[:, j * HD : (j + 1) * HD]

    def gain_copy(to, owner):
        return rcopy(gain_s, gain_c.at[owner], gain_ss.at[to], gain_rs.at[owner], {"ctx": to})

    loop(1, nctx, lambda i: gain_copy((c + i) % nctx, c).start())
    gain_c[c] = gain_s[...]

    mark("return_ffn")
    return_send(1, 3)

    mark("backward")
    def go_copy(n, src, dst, to, owner):
        return rcopy(src.at[at(to * T, T)], dst.at[:, at(owner * HD, HD)], go_ss.at[n, to], go_rs.at[n, owner], {"ctx": to})

    loop(1, nctx, lambda i: gr_copy((c + i) % nctx, (c + i) % nctx, (c + i) % nctx).wait_recv())
    mark("grad_values")
    gvsend[...] = dot_nn(probs_h[...], grh[...]).astype(BF16)
    loop(1, nctx, lambda i: go_copy(2, gvsend, gv_hbm, (c + i) % nctx, c).start())
    mark("gain")

    loop(1, nctx, lambda i: gain_copy((c + i) % nctx, (c + i) % nctx).wait_recv())
    gain_l_s[...] = jnp.sum(gain_c[...], axis=0)

    def gainl_copy(to, owner):
        return rcopy(gain_l_s, gain_l.at[owner], gainl_ss.at[to], gainl_rs.at[owner], {"lang": to})

    loop(1, nlang, lambda i: gainl_copy((me + i) % nlang, me).start())
    gain_l[me] = gain_l_s[...]
    mark("backward_loop")

    def backward(i):
        p = (c + 1 + i) % nctx
        probs = probs_t[at(p * L, L), :]
        gp = dot_nt(vh[...], grh[at(p * T, T), :])
        gs = (probs * (gp - jnp.sum(probs * gp, axis=0, keepdims=True))).astype(BF16)
        probs_h[:, at(p * T, T)] = gs
        gqsend[at(p * T, T), :] = (dot_nn(jnp.transpose(gs), kh[...]) * scale).astype(BF16)

        @pl.when(i < nctx - 1)
        def _():
            go_copy(0, gqsend, gq_hbm, p, c).start()

    loop(0, nctx, backward)
    mark("send_keys")
    gksend[...] = (dot_nn(probs_h[...], qh[...]) * scale).astype(BF16)
    loop(1, nctx, lambda i: go_copy(1, gksend, gk_hbm, (c + i) % nctx, c).start())
    triples = ((gqsend, gq_hbm), (gksend, gk_hbm), (gvsend, gv_hbm))
    own_out = [
        pltpu.make_async_copy(src.at[at(c * T, T)], dst.at[:, at(c * HD, HD)], loc_sem.at[3 + n])
        for n, (src, dst) in enumerate(triples)
    ]
    for copy in own_out:
        copy.start()

    mark("combine_ffn")
    combine(3)
    layer_out[...] = (summed_s[...] + gn_s[...]).astype(BF16)

    mark("gain_wait")
    loop(1, nlang, lambda i: gainl_copy((me + i) % nlang, (me + i) % nlang).wait_recv())
    grad_gain[...] = jnp.sum(gain_l[...], axis=0)

    mark("wait_out")
    def wait_out(i):
        p = (c + i) % nctx
        for n, (src, dst) in enumerate(triples):
            go_copy(n, src, dst, p, p).wait_recv()

    loop(1, nctx, wait_out)

    mark("wait_sent")
    def sent_ctx(i):
        p = (c + i) % nctx
        for n in range(4):
            in_copy(n, p, c).wait_send()
        rcopy(attsend.at[at(p * T, T)], att.at[:, at(c * HD, HD)], att_ss.at[p], att_rs.at[c], {"ctx": p}).wait_send()
        gr_copy(p, c, p).wait_send()
        gain_copy(p, c).wait_send()
        for n, (src, dst) in enumerate(triples):
            go_copy(n, src, dst, p, c).wait_send()

    loop(1, nctx, sent_ctx)

    def sent_lang(d):
        for phase in range(4):
            rcopy(
                msg_s.at[phase, at(d * MR, MR)],
                msg_r.at[phase, at(d * MR, MR)],
                lang_ss.at[phase, d],
                lang_rs.at[phase, d],
                {"lang": (me + d) % nlang},
            ).wait_send()
        gainl_copy((me + d) % nlang, me).wait_send()

    loop(1, nlang, sent_lang)

    for w, buf in ((0, rows_g), (1, rows_n)):
        for g in range(GROUPS):
            for side in range(2):
                near_copy(w, buf, g, side).wait_send()
                half_copy(w, buf, g, side).wait_send()
                mid_copy(w, g, side).wait_send()
                for h in range(2):
                    fin_copy(w, g, side, h).wait_send()
            for what in range(5):
                sib_copy(w, buf, g, what).wait_send()

    def sent_pair(i):
        for w in range(2):
            for g in range(GROUPS):
                pair_copy(w, i, g).wait_send()

    loop(0, X, sent_pair)
    for copy in own_out:
        copy.wait()
    for copy in out_w:
        copy.wait()
    mark(None)


def store(*refs):
    n = (len(refs) - 2) // 3
    fetch_sem, store_sem = refs[-2:]
    fetches = [pltpu.make_async_copy(refs[i], refs[2 * n + i], fetch_sem.at[i]) for i in range(n)]
    stores = [pltpu.make_async_copy(refs[2 * n + i], refs[n + i], store_sem.at[i]) for i in range(n)]
    for copy in fetches:
        copy.start()
    for fetch, copy in zip(fetches, stores):
        fetch.wait()
        copy.start()
    for copy in stores:
        copy.wait()


def local(
    attn_queries,
    attn_keys,
    attn_values,
    residual,
    cotangent,
    segment_ids,
    language_ids,
    token_counts,
    norm_gain,
    gate_weight,
    up_weight,
    down_weight,
):
    nctx = lax.axis_size("ctx")
    nlang = lax.axis_size("lang")
    T, D = attn_queries.shape[1:]
    F = gate_weight.shape[2]
    L = nctx * T
    J = D // HD
    X = nctx // 2
    MR = PITCH * J
    LG = nlang // GROUPS
    RG = LG * CAP
    BR = nlang * CAP
    R = nctx * BR
    vmem = lambda *shape: pltpu.VMEM(shape, BF16)
    vmem32 = lambda *shape: pltpu.VMEM(shape, F32)
    dma = lambda *shape: pltpu.SemaphoreType.DMA(shape)
    scratch = [
        vmem(L, HD),
        vmem(L, HD),
        vmem(L, HD),
        vmem(16, T),
        vmem(16, L),
        vmem32(L, T),
        vmem32(nctx * L, T),
        vmem(L, L),
        vmem(L, HD),
        vmem(T, D),
        vmem(D, F),
        vmem(D, F),
        vmem(F, D),
        vmem(D, F),
        vmem(D, F),
        vmem(F, D),
        vmem32(T, D),
        vmem32(T, D),
        vmem32(T, D),
        vmem32(T, D),
        vmem(J * T, HD),
        vmem(nlang * MR, J * T),
        vmem(J * T, nlang * MR),
        vmem(J * RG, LG * MR),
        vmem(LG * MR, J * 128),
        vmem(J * 128, HD),
        vmem(4, nlang * MR, HD),
        vmem(4, nlang * MR, HD),
        vmem(R, D),
        vmem(R, D),
        vmem32(R, F),
        vmem(R, F),
        vmem(R, F),
        vmem(R, F),
        vmem(2, R, D),
        vmem(2, X * BR, D),
        vmem(2, X * BR, D),
        vmem(2, BR, D),
        vmem(2, 2 * BR, D),
        vmem(T, D),
        vmem(L, HD),
        vmem(L, HD),
        vmem(L, HD),
        vmem(L, HD),
        vmem32(J, HD),
        vmem32(nctx, J, HD),
        vmem32(J, HD),
        vmem32(nlang, J, HD),
        dma(6),
        dma(3),
        dma(4, nctx),
        dma(4, nctx),
        dma(nctx),
        dma(nctx),
        dma(4, nlang),
        dma(4, nlang),
        dma(2 * GROUPS, 2),
        dma(2 * GROUPS, 2),
        dma(2 * GROUPS, 2),
        dma(2 * GROUPS, 2),
        dma(2 * GROUPS, 5),
        dma(2 * GROUPS, 5),
        dma(2, X * GROUPS),
        dma(2, X * GROUPS),
        dma(2 * GROUPS, 2),
        dma(2 * GROUPS, 2),
        dma(2 * GROUPS, 4),
        dma(2 * GROUPS, 4),
        dma(nctx),
        dma(nctx),
        dma(3, nctx),
        dma(3, nctx),
        dma(nctx),
        dma(nctx),
        dma(nlang),
        dma(nlang),
    ]
    anywhere = pl.BlockSpec(memory_space=pl.ANY)
    inside = pl.BlockSpec(memory_space=pltpu.VMEM)
    shape = lambda *dims: jax.ShapeDtypeStruct(dims, BF16)
    outs = pl.pallas_call(
        functools.partial(kernel, nctx, nlang),
        out_shape=(
            shape(T, D),
            shape(T, D),
            shape(T, D),
            shape(T, D),
            shape(T, D),
            jax.ShapeDtypeStruct((J, HD), F32),
            shape(D, F),
            shape(D, F),
            shape(F, D),
        ),
        in_specs=[anywhere] * 3 + [inside] * 6 + [anywhere] * 3,
        out_specs=(inside, anywhere, anywhere, anywhere, inside, inside, anywhere, anywhere, anywhere),
        scratch_shapes=scratch,
        compiler_params=pltpu.CompilerParams(collective_id=0, has_side_effects=True, vmem_limit_bytes=58 * 1024 * 1024),
        cost_estimate=pl.CostEstimate(flops=16_000_000_000, bytes_accessed=10_000_000, transcendentals=3_000_000),
        name="layer",
    )(
        attn_queries[0],
        attn_keys[0],
        attn_values[0],
        residual[0],
        cotangent[0],
        segment_ids,
        language_ids.reshape(1, T),
        token_counts.reshape(1, nlang),
        norm_gain.reshape(1, D),
        gate_weight[0],
        up_weight[0],
        down_weight[0],
    )
    outs = pl.pallas_call(
        store,
        out_shape=tuple(jax.ShapeDtypeStruct(o.shape, o.dtype) for o in outs),
        in_specs=[anywhere] * len(outs),
        out_specs=(anywhere,) * len(outs),
        scratch_shapes=[pltpu.VMEM(o.shape, o.dtype) for o in outs] + [dma(len(outs)), dma(len(outs))],
        compiler_params=pltpu.CompilerParams(vmem_limit_bytes=58 * 1024 * 1024),
        name="store",
    )(*outs)
    layer_out, gq, gk, gv, gres, ggain, gwg, gwu, gwd = outs
    return (
        layer_out[None],
        gq[None],
        gk[None],
        gv[None],
        gres[None],
        ggain.reshape(D),
        gwg[None],
        gwu[None],
        gwd[None],
    )


def solution(mesh):
    block = P("lang", "ctx", None)
    in_specs = (
        block,
        block,
        block,
        block,
        block,
        P("lang", "ctx"),
        block,
        P(),
        P(),
        P("lang", None, "ctx"),
        P("lang", None, "ctx"),
        block,
    )
    out_specs = (
        block,
        block,
        block,
        block,
        block,
        P(),
        P("lang", None, "ctx"),
        P("lang", None, "ctx"),
        block,
    )
    return jax.shard_map(local, mesh=mesh, in_specs=in_specs, out_specs=out_specs, check_vma=False)
```

```python
import functools

import jax
import jax.numpy as jnp
from jax import lax
from jax.experimental import pallas as pl
from jax.experimental.pallas import tpu as pltpu
from jax.sharding import PartitionSpec as P

HD = 128
EPSILON = 1e-06
CAP = 5
PITCH = 6
GROUPS = 2
MESH = pl.DeviceIdType.MESH
F32 = jnp.float32
BF16 = jnp.bfloat16
MASKED = -1e30


def dot_nn(a, b):
    return lax.dot_general(a, b, (((1,), (0,)), ((), ())), preferred_element_type=F32)


def dot_nt(a, b):
    return lax.dot_general(a, b, (((1,), (1,)), ((), ())), preferred_element_type=F32)


def at(start, size, step=None):
    return pl.ds(pl.multiple_of(start, step or size), size)


def kernel(
    nctx,
    nlang,
    q_hbm,
    k_hbm,
    v_hbm,
    residual,
    cotangent,
    segment,
    language,
    counts,
    gain,
    wg_hbm,
    wu_hbm,
    wd_hbm,
    layer_out,
    gq_hbm,
    gk_hbm,
    gv_hbm,
    grad_res,
    grad_gain,
    gwg_hbm,
    gwu_hbm,
    gwd_hbm,
    qh,
    kh,
    vh,
    segsend,
    segrow,
    segcol,
    probs_t,
    probs_h,
    kh_t,
    attsend,
    att,
    wg,
    wu,
    wd,
    gwg,
    gwu,
    gwd,
    summed_s,
    normed_s,
    gout_s,
    gn_s,
    stack,
    sel,
    sel_t,
    spread,
    spread_t,
    stack_r,
    msg_s,
    msg_r,
    rows_n,
    rows_g,
    gh_s,
    hid_s,
    ggp_s,
    gup_s,
    part,
    pair_r,
    sum_s,
    mid_r,
    fin_r,
    grsend,
    grh,
    gqsend,
    gksend,
    gvsend,
    gain_s,
    gain_c,
    gain_l_s,
    gain_l,
    loc_sem,
    out_sem,
    in_s,
    in_r,
    att_ss,
    att_rs,
    lang_ss,
    lang_rs,
    near_ss,
    near_rs,
    half_ss,
    half_rs,
    sib_ss,
    sib_rs,
    pair_ss,
    pair_rs,
    mid_ss,
    mid_rs,
    fin_ss,
    fin_rs,
    gr_ss,
    gr_rs,
    go_ss,
    go_rs,
    gain_ss,
    gain_rs,
    gainl_ss,
    gainl_rs,
):
    T, D = residual.shape
    L = nctx * T
    J = D // HD
    X = nctx // 2
    assert X == 4
    F = wg.shape[1]
    H = D // 2
    MR = PITCH * J
    LG = nlang // GROUPS
    RG = LG * CAP
    OP = 128
    scale = HD ** (-0.5)
    c = lax.axis_index("ctx")
    me = lax.axis_index("lang")
    x = c // 2
    core = c % 2
    sib = x * 2 + 1 - core
    right, left, across = (x + 1) % X, (x + 3) % X, (x + 2) % X

    def rcopy(src, dst, ssem, rsem, dev):
        return pltpu.make_async_remote_copy(
            src_ref=src, dst_ref=dst, send_sem=ssem, recv_sem=rsem, device_id=dev, device_id_type=MESH
        )

    def each(lo, hi, body):
        for i in range(lo, hi):
            body(i)

    def loop(lo, hi, body, unroll=1):
        def step(i, carry):
            body(i)
            return carry

        lax.fori_loop(lo, hi, step, 0, unroll=unroll)

    scope = []

    def mark(name):
        if scope:
            scope.pop().__exit__(None, None, None)
        if name:
            scope.append(jax.named_scope(name))
            scope[-1].__enter__()

    mark("entry")
    weight_in = [
        pltpu.make_async_copy(src, dst, loc_sem.at[i])
        for i, (src, dst) in enumerate(((wd_hbm, wd), (wg_hbm, wg), (wu_hbm, wu)))
    ]
    own_in = [
        pltpu.make_async_copy(src.at[:, at(c * HD, HD)], dst.at[at(c * T, T)], loc_sem.at[3 + i])
        for i, (src, dst) in enumerate(((k_hbm, kh), (q_hbm, qh), (v_hbm, vh)))
    ]
    segsend[...] = jnp.broadcast_to(segment[...].astype(F32), segsend.shape).astype(BF16)

    barrier = pltpu.get_barrier_semaphore()
    loop(1, nctx, lambda i: pl.semaphore_signal(barrier, inc=1, device_id={"ctx": lax.rem(c + i, nctx)}, device_id_type=MESH))
    loop(1, nlang, lambda i: pl.semaphore_signal(barrier, inc=1, device_id={"lang": lax.rem(me + i, nlang)}, device_id_type=MESH))
    for copy in own_in:
        copy.start()
    pl.semaphore_wait(barrier, nctx - 1 + nlang - 1)

    mark("send_qkv")
    def in_copy(i, to, owner):
        if i == 3:
            src, dst = segsend, segrow.at[:, at(owner * T, T)]
        else:
            src, dst = ((k_hbm, kh), (q_hbm, qh), (v_hbm, vh))[i]
            src, dst = src.at[:, at(to * HD, HD)], dst.at[at(owner * T, T)]
        return rcopy(src, dst, in_s.at[i, to], in_r.at[i, owner], {"ctx": to})

    for which in ((3, 0), (1,), (2,)):

        def send_in(i):
            for n in which:
                in_copy(n, lax.rem(c + i, nctx), c).start()

        each(1, nctx, send_in)
    for copy in weight_in:
        copy.start()
    segrow[:, at(c * T, T)] = segsend[...]

    mark("slots")
    lang_row = language[...].astype(F32)
    lang_col = jnp.transpose(jnp.broadcast_to(lang_row, (T, T)))
    earlier = lax.broadcasted_iota(jnp.int32, (T, T), 0) < lax.broadcasted_iota(jnp.int32, (T, T), 1)
    rank = jnp.sum(jnp.where((lang_col == lang_row) & earlier, 1.0, 0.0), axis=0, keepdims=True)
    slot_row = lang_row * float(MR) + rank
    slot_col = jnp.transpose(jnp.broadcast_to(slot_row, (T, T)))[:, 0:1].astype(jnp.int32)
    slot_row = slot_row.astype(jnp.int32)
    for j in range(J):
        hit = lax.broadcasted_iota(jnp.int32, (nlang * MR, T), 0) == slot_row + PITCH * j
        sel[:, j * T : (j + 1) * T] = jnp.where(hit, 1.0, 0.0).astype(BF16)

    lang_hit = lang_col[:, 0:1] == lax.broadcasted_iota(jnp.int32, (T, nlang), 1).astype(F32)
    count = jnp.sum(jnp.where(lang_hit, counts[...].astype(F32), 0.0), axis=1, keepdims=True)
    gout_s[...] = cotangent[...].astype(F32) * (16.0 * lax.rsqrt(count))

    NY = 4 if nlang % 8 == 0 else 1
    NZ = nlang // NY
    me_z, me_y = lax.div(me, NY), lax.rem(me, NY)

    def partner(d, sign):
        if NY == 1:
            return lax.rem(me + nlang + sign * d, nlang)
        turn_z = d // NY
        off_z = (2 * turn_z) % NZ + turn_z // (NZ // 2)
        return lax.rem(me_z + NZ + sign * off_z, NZ) * NY + lax.rem(me_y + NY + sign * (d % NY), NY)

    def dispatch(phase, stacked):
        for j in range(J):
            stack[j * T : (j + 1) * T, :] = stacked[:, j * HD : (j + 1) * HD]
        msg_s[phase] = dot_nn(sel[...], stack[...]).astype(BF16)

        def one(d):
            to = partner(d, 1)
            rcopy(
                msg_s.at[phase, at(to * MR, MR)],
                msg_r.at[phase, at(d * MR, MR)],
                lang_ss.at[phase, d],
                lang_rs.at[phase, d],
                {"lang": to},
            ).start()

        each(1, nlang, one)
        msg_r[phase, 0:MR, :] = msg_s[phase, at(me * MR, MR), :]

    def lang_wait(phase, lo, hi):
        def one(d):
            rcopy(
                msg_s.at[phase, at(d * MR, MR)],
                msg_r.at[phase, at(d * MR, MR)],
                lang_ss.at[phase, d],
                lang_rs.at[phase, d],
                {"lang": me},
            ).wait_recv()

        each(lo, hi, one)

    def lang_wait_but_own(phase):
        def one(d):
            l = lax.rem(me + d, nlang)
            rcopy(
                msg_s.at[phase, at(l * MR, MR)],
                msg_r.at[phase, at(l * MR, MR)],
                lang_ss.at[phase, d],
                lang_rs.at[phase, l],
                {"lang": me},
            ).wait_recv()

        each(1, nlang, one)

    mark("dispatch_grads")
    dispatch(0, gout_s[...].astype(BF16))

    mark("spread")
    o_col = lax.broadcasted_iota(jnp.int32, (RG, LG * MR), 0)
    base = ((o_col * 205) >> 10) * (MR - CAP) + o_col
    for j in range(J):
        hit = lax.broadcasted_iota(jnp.int32, (RG, LG * MR), 1) == base + PITCH * j
        spread[j * RG : (j + 1) * RG, :] = jnp.where(hit, 1.0, 0.0).astype(BF16)

    mark("wait_qkv")
    for copy in own_in:
        copy.wait()

    def wait_in(n):
        each(1, nctx, lambda i: in_copy(n, lax.rem(c + i, nctx), lax.rem(c + i, nctx)).wait_recv())

    for n in (3, 0):
        wait_in(n)
    for p in range(nctx):
        row = segrow[0:1, p * T : (p + 1) * T].astype(F32)
        segcol[p * T : (p + 1) * T, :] = jnp.transpose(jnp.broadcast_to(row, (T, T)))

    mark("attention")
    def forward(i):
        p = lax.rem(c + nctx - i, nctx)
        s = dot_nt(qh[at(p * T, T), :], kh[...]) * scale
        same = segcol[at(p * T, T), 0:1] == segrow[0:1, :].astype(F32)
        s = jnp.where(same, s, MASKED)
        e = jnp.exp(s - jnp.max(s, axis=1, keepdims=True))
        probs_h[at(p * T, T), :] = (e / jnp.sum(e, axis=1, keepdims=True)).astype(BF16)

    def wait_query(i):
        p = lax.rem(c + nctx - i, nctx)
        in_copy(1, p, p).wait_recv()

    BATCH = nctx // 2
    for first in range(0, nctx, BATCH):
        each(max(1, first), first + BATCH, wait_query)
        loop(first, first + BATCH, forward, BATCH)
    mark("wait_values")
    wait_in(2)
    mark("attended")

    attsend[...] = dot_nn(probs_h[...], vh[...]).astype(BF16)

    def send_attended(i):
        p = lax.rem(c + i, nctx)
        rcopy(attsend.at[at(p * T, T)], att.at[:, at(c * HD, HD)], att_ss.at[p], att_rs.at[c], {"ctx": p}).start()

    each(1, nctx, send_attended)
    att[:, at(c * HD, HD)] = attsend[at(c * T, T), :]

    def block(chip, g, k):
        return at(((chip * GROUPS + g) * 2 + k) * RG, RG, 16)

    def near_copy(w, buf, g, side):
        rows = block(x, g, core)
        to = (right, left)[side] * 2 + core
        n = w * GROUPS + g
        return rcopy(buf.at[rows], buf.at[rows], near_ss.at[n, side], near_rs.at[n, side], {"ctx": to})

    def half_copy(w, buf, g, side):
        rows = block((left, right)[side], g, core)
        cols = slice(side * H, (side + 1) * H)
        to = (right, left)[side] * 2 + core
        n = w * GROUPS + g
        return rcopy(buf.at[rows, cols], buf.at[rows, cols], half_ss.at[n, side], half_rs.at[n, side], {"ctx": to})

    def sib_copy(w, buf, g, what, k=core):
        n = w * GROUPS + g
        rows = block((x, left, right, across, across)[what], g, k)
        cols = slice(None) if what < 3 else slice((what - 3) * H, (what - 2) * H)
        return rcopy(buf.at[rows, cols], buf.at[rows, cols], sib_ss.at[n, what], sib_rs.at[n, what], {"ctx": sib})

    def gather_send(w, buf, phase, g):
        lang_wait(phase, max(1, g * LG), (g + 1) * LG)
        rows = block(x, g, core)
        for j in range(J):
            buf[rows, j * HD : (j + 1) * HD] = dot_nn(
                spread[j * RG : (j + 1) * RG, :], msg_r[phase, g * LG * MR : (g + 1) * LG * MR, :]
            ).astype(BF16)
        near_copy(w, buf, g, 0).start()
        near_copy(w, buf, g, 1).start()
        sib_copy(w, buf, g, 0).start()

    def near_forward(w, buf, g):
        for side in range(2):
            rows = block((left, right)[side], g, core)
            n = w * GROUPS + g
            rcopy(buf.at[rows], buf.at[rows], near_ss.at[n, side], near_rs.at[n, side], {"ctx": sib}).wait_recv()
            half_copy(w, buf, g, side).start()
            sib_copy(w, buf, g, 1 + side).start()

    def half_forward(w, buf, g):
        for side in range(2):
            rows = block(across, g, core)
            cols = slice(side * H, (side + 1) * H)
            n = w * GROUPS + g
            rcopy(
                buf.at[rows, cols], buf.at[rows, cols], half_ss.at[n, side], half_rs.at[n, side], {"ctx": sib}
            ).wait_recv()
            sib_copy(w, buf, g, 3 + side).start()

    def sib_wait(w, buf, g, what):
        sib_copy(w, buf, g, what, 1 - core).wait_recv()

    mark("grad_rows")
    for g in range(GROUPS):
        gather_send(0, rows_g, 0, g)

    mark("wait_attended")
    def wait_att(i):
        p = lax.rem(c + i, nctx)
        rcopy(attsend.at[at(p * T, T)], att.at[:, at(p * HD, HD)], att_ss.at[p], att_rs.at[p], {"ctx": p}).wait_recv()

    each(1, nctx, wait_att)
    mark("norm_dispatch")
    summed = residual[...].astype(F32) + att[...].astype(F32)
    summed_s[...] = summed
    inv_rms = lax.rsqrt(jnp.mean(summed * summed, axis=1, keepdims=True) + EPSILON)
    normed = summed * inv_rms
    normed_s[...] = normed
    dispatch(1, (normed * gain[...]).astype(BF16))

    mark("layouts")
    for j in range(J):
        hit = lax.broadcasted_iota(jnp.int32, (T, nlang * MR), 1) == slot_col + PITCH * j
        sel_t[j * T : (j + 1) * T, :] = jnp.where(hit, 1.0, 0.0).astype(BF16)
    o_row = lax.broadcasted_iota(jnp.int32, (LG * MR, OP), 1)
    base_row = ((o_row * 205) >> 10) * (MR - CAP) + o_row
    inside = o_row < RG
    for j in range(J):
        hit = (lax.broadcasted_iota(jnp.int32, (LG * MR, OP), 0) == base_row + PITCH * j) & inside
        spread_t[:, j * OP : (j + 1) * OP] = jnp.where(hit, 1.0, 0.0).astype(BF16)
    stack_r[...] = jnp.zeros_like(stack_r)

    mark("back_probs")

    def back_probs(p):
        s = dot_nt(kh[...], qh[at(p * T, T), :]) * scale
        same = segcol[...] == segrow[0:1, at(p * T, T)].astype(F32)
        s = jnp.where(same, s, MASKED)
        e = jnp.exp(s - jnp.max(s, axis=0, keepdims=True))
        probs = e / jnp.sum(e, axis=0, keepdims=True)
        probs_t[at(p * L, L), :] = probs
        probs_h[:, at(p * T, T)] = probs.astype(BF16)

    loop(0, nctx, back_probs, BATCH)
    kh_t[...] = jnp.transpose(kh[...])
    mark("forward_grads")
    for g in range(GROUPS):
        near_forward(0, rows_g, g)
    mark("norm_rows")
    for g in range(GROUPS):
        gather_send(1, rows_n, 1, g)
        half_forward(0, rows_g, g)
    mark("grad_hidden")
    weight_in[0].wait()
    CR = GROUPS * 2 * RG
    for g in range(GROUPS):
        for what in range(5):
            sib_wait(0, rows_g, g, what)

    def grad_hidden(i):
        rows = at(i * CR, CR, 16)
        gh_s[rows, :] = dot_nt(rows_g[rows, :], wd[...])

    loop(0, X, grad_hidden)
    weight_in[1].wait()
    weight_in[2].wait()

    FT = min(F, 256)
    DT = min(D, 512)

    def flat(chip, g):
        return at((chip * GROUPS + g) * RG, RG, 16)

    def pair_copy(w, chip, g):
        n = chip * GROUPS + g
        return rcopy(
            part.at[w, block(chip, g, 1 - core)], pair_r.at[w, flat(chip, g)], pair_ss.at[w, n], pair_rs.at[w, n], {"ctx": sib}
        )

    def pair_sum(w, chip, g, cols):
        own = part[w, block(chip, g, core), cols].astype(F32)
        return own + pair_r[w, flat(chip, g), cols].astype(F32)

    halves = (slice(0, H), slice(H, D))

    def mid_copy(w, g, h):
        to = (right, left)[h] * 2 + core
        src = sum_s.at[w, flat(across, g), halves[h]]
        n = w * GROUPS + g
        return rcopy(src, mid_r.at[w, at(g * RG, RG, 16), halves[h]], mid_ss.at[n, h], mid_rs.at[n, h], {"ctx": to})

    def fin_copy(w, g, side, h):
        chip = (right, left)[side]
        src = sum_s.at[w, flat(chip, g), halves[h]]
        dst = fin_r.at[w, at((side * GROUPS + g) * RG, RG, 16), halves[h]]
        n = w * GROUPS + g
        return rcopy(src, dst, fin_ss.at[n, side * 2 + h], fin_rs.at[n, side * 2 + h], {"ctx": chip * 2 + core})

    def sum_across(w, g):
        pair_copy(w, across, g).wait_recv()
        for h in range(2):
            sum_s[w, flat(across, g), halves[h]] = pair_sum(w, across, g, halves[h]).astype(BF16)
            mid_copy(w, g, h).start()

    def sum_near(w, g, side):
        chip, h = (right, left)[side], 1 - side
        pair_copy(w, chip, g).wait_recv()
        sum_s[w, flat(chip, g), halves[h]] = pair_sum(w, chip, g, halves[h]).astype(BF16)
        fin_copy(w, g, side, h).start()

    def sum_late(w, g):
        for side in range(2):
            chip, h = (right, left)[side], side
            mid_copy(w, g, h).wait_recv()
            total = pair_sum(w, chip, g, halves[h]) + mid_r[w, at(g * RG, RG, 16), halves[h]].astype(F32)
            sum_s[w, flat(chip, g), halves[h]] = total.astype(BF16)
            fin_copy(w, g, side, h).start()

    def sum_own(w, g):
        pair_copy(w, x, g).wait_recv()
        for side in range(2):
            for h in range(2):
                fin_copy(w, g, side, h).wait_recv()
        total = pair_sum(w, x, g, slice(None))
        for side in range(2):
            total = total + fin_r[w, at((side * GROUPS + g) * RG, RG, 16), :].astype(F32)
        return total.astype(BF16)

    def feed(rows):
        for n in range(F // FT):
            cols = slice(n * FT, (n + 1) * FT)
            pre_gate = dot_nn(rows_n[rows, :], wg[:, cols])
            pre_up = dot_nn(rows_n[rows, :], wu[:, cols])
            gh = gh_s[rows, cols]
            sig = jax.nn.sigmoid(pre_gate)
            silu = pre_gate * sig
            hid_s[rows, cols] = (silu * pre_up).astype(BF16)
            ggp_s[rows, cols] = (gh * pre_up * sig * (1.0 + pre_gate * (1.0 - sig))).astype(BF16)
            gup_s[rows, cols] = (gh * silu).astype(BF16)
        for n in range(D // DT):
            cols = slice(n * DT, (n + 1) * DT)
            part[0, rows, cols] = (dot_nt(ggp_s[rows, :], wg[cols, :]) + dot_nt(gup_s[rows, :], wu[cols, :])).astype(BF16)

    def feed_chip(i):
        chip = (x + i + i // 2) % X
        for g in range(GROUPS):
            for what, when in ((0, 0), (2, 1), (1, 2)):

                @pl.when(i == when)
                def _():
                    sib_wait(1, rows_n, g, what)

        feed(at(chip * CR, CR, 16))
        for g in range(GROUPS):
            pair_copy(0, chip, g).start()

    mark("feed_own")
    loop(0, 1, feed_chip)
    mark("feed_near_wait")
    for g in range(GROUPS):
        near_forward(1, rows_n, g)
    mark("feed_near")
    loop(1, 3, feed_chip)
    mark("sum_near")
    for g in range(GROUPS):
        for side in range(2):
            sum_near(0, g, side)
    for g in range(GROUPS):
        half_forward(1, rows_n, g)
    mark("feed_across")

    def feed_across(g):
        for m in range(GROUPS):

            @pl.when(g == m)
            def _():
                sib_wait(1, rows_n, m, 3)
                sib_wait(1, rows_n, m, 4)

        feed(at((across * GROUPS + g) * 2 * RG, 2 * RG, 16))
        pair_copy(0, across, g).start()

    loop(0, GROUPS, feed_across)
    mark("sum_across")
    for g in range(GROUPS):
        sum_across(0, g)

    mark("down")

    def down(i):
        rows = at(i * CR, CR, 16)
        part[1, rows, :] = dot_nn(hid_s[rows, :], wd[...]).astype(BF16)
        for g in range(GROUPS):
            pair_copy(1, i, g).start()

    loop(0, X, down)
    mark("sum_late")
    for g in range(GROUPS):
        sum_late(0, g)

    def grad_w(n):
        cols = at(n * FT, FT)
        turned = jnp.transpose(rows_n[:, cols])
        gwg[cols, :] = dot_nn(turned, ggp_s[...]).astype(BF16)
        gwu[cols, :] = dot_nn(turned, gup_s[...]).astype(BF16)

    def grad_wd(n):
        cols = at(n * FT, FT)
        gwd[cols, :] = dot_nn(jnp.transpose(hid_s[:, cols]), rows_g[...]).astype(BF16)

    def return_send(w, phase):
        for g in range(GROUPS):
            total = sum_own(w, g)
            for j in range(J):
                stack_r[j * OP : j * OP + RG, :] = total[:, j * HD : (j + 1) * HD]
            msg_s[phase, g * LG * MR : (g + 1) * LG * MR, :] = dot_nn(spread_t[...], stack_r[...]).astype(BF16)

            def one(d):
                to = partner(d, -1)
                rcopy(
                    msg_s.at[phase, at(d * MR, MR)],
                    msg_r.at[phase, at(me * MR, MR)],
                    lang_ss.at[phase, d],
                    lang_rs.at[phase, me],
                    {"lang": to},
                ).start()

            each(max(1, g * LG), (g + 1) * LG, one)
        msg_r[phase, at(me * MR, MR), :] = msg_s[phase, 0:MR, :]

    def combine(phase):
        lang_wait_but_own(phase)
        for j in range(J):
            gn_s[:, j * HD : (j + 1) * HD] = dot_nn(sel_t[j * T : (j + 1) * T, :], msg_r[phase])

    mark("grad_w_a")
    half = max(1, (D // FT) // 2)
    loop(0, half, grad_w)
    mark("return_grads")
    return_send(0, 2)
    mark("ffn_sums")
    for g in range(GROUPS):
        sum_across(1, g)
    for g in range(GROUPS):
        for side in range(2):
            sum_near(1, g, side)
    mark("grad_w_b")
    loop(half, D // FT, grad_w)
    mark("ffn_late")
    for g in range(GROUPS):
        sum_late(1, g)
    mark("grad_wd")
    out_w = [
        pltpu.make_async_copy(src, dst, out_sem.at[i])
        for i, (src, dst) in enumerate(((gwg, gwg_hbm), (gwu, gwu_hbm), (gwd, gwd_hbm)))
    ]
    out_w[0].start()
    out_w[1].start()
    loop(0, F // FT, grad_wd)
    out_w[2].start()

    mark("combine_grads")
    combine(2)
    mark("grad_residual")
    grad_normin = gn_s[...]
    normed = normed_s[...]
    summed = summed_s[...]
    inv_rms = lax.rsqrt(jnp.mean(summed * summed, axis=1, keepdims=True) + EPSILON)
    scaled = grad_normin * gain[...]
    gres = gout_s[...] + inv_rms * (scaled - normed * jnp.mean(scaled * normed, axis=1, keepdims=True))
    grsend[...] = gres.astype(BF16)

    def gr_copy(to, owner, sem_at):
        return rcopy(grsend.at[:, at(to * HD, HD)], grh.at[at(owner * T, T)], gr_ss.at[sem_at], gr_rs.at[owner], {"ctx": to})

    each(1, nctx, lambda i: gr_copy(lax.rem(c + i, nctx), c, lax.rem(c + i, nctx)).start())
    grh[at(c * T, T), :] = grsend[:, at(c * HD, HD)]
    grad_res[...] = grsend[...]
    gain_part = jnp.sum(grad_normin * normed, axis=0, keepdims=True)
    for j in range(J):
        gain_s[j : j + 1, :] = gain_part[:, j * HD : (j + 1) * HD]

    def gain_copy(to, owner):
        return rcopy(gain_s, gain_c.at[owner], gain_ss.at[to], gain_rs.at[owner], {"ctx": to})

    each(1, nctx, lambda i: gain_copy(lax.rem(c + i, nctx), c).start())
    gain_c[c] = gain_s[...]

    mark("return_ffn")
    return_send(1, 3)

    mark("backward")
    def go_copy(n, src, dst, to, owner):
        return rcopy(src.at[at(to * T, T)], dst.at[:, at(owner * HD, HD)], go_ss.at[n, to], go_rs.at[n, owner], {"ctx": to})

    each(1, nctx, lambda i: gr_copy(lax.rem(c + i, nctx), lax.rem(c + i, nctx), lax.rem(c + i, nctx)).wait_recv())
    mark("grad_values")
    gvsend[...] = dot_nn(probs_h[...], grh[...]).astype(BF16)
    each(1, nctx, lambda i: go_copy(2, gvsend, gv_hbm, lax.rem(c + i, nctx), c).start())
    mark("gain")

    each(1, nctx, lambda i: gain_copy(lax.rem(c + i, nctx), lax.rem(c + i, nctx)).wait_recv())
    gain_l_s[...] = jnp.sum(gain_c[...], axis=0)

    def gainl_copy(to, owner):
        return rcopy(gain_l_s, gain_l.at[owner], gainl_ss.at[to], gainl_rs.at[owner], {"lang": to})

    each(1, nlang, lambda i: gainl_copy(lax.rem(me + i, nlang), me).start())
    gain_l[me] = gain_l_s[...]
    mark("backward_loop")

    def backward(i):
        p = lax.rem(c + 1 + i, nctx)
        probs = probs_t[at(p * L, L), :]
        gp = dot_nt(vh[...], grh[at(p * T, T), :])
        gs = (probs * (gp - jnp.sum(probs * gp, axis=0, keepdims=True))).astype(BF16)
        probs_h[:, at(p * T, T)] = gs
        gqsend[at(p * T, T), :] = jnp.transpose(dot_nn(kh_t[...], gs) * scale).astype(BF16)

        @pl.when(i < nctx - 1)
        def _():
            go_copy(0, gqsend, gq_hbm, p, c).start()

    loop(0, nctx, backward, BATCH)
    mark("send_keys")
    gksend[...] = (dot_nn(probs_h[...], qh[...]) * scale).astype(BF16)
    each(1, nctx, lambda i: go_copy(1, gksend, gk_hbm, lax.rem(c + i, nctx), c).start())
    triples = ((gqsend, gq_hbm), (gksend, gk_hbm), (gvsend, gv_hbm))
    own_out = [
        pltpu.make_async_copy(src.at[at(c * T, T)], dst.at[:, at(c * HD, HD)], loc_sem.at[3 + n])
        for n, (src, dst) in enumerate(triples)
    ]
    for copy in own_out:
        copy.start()

    mark("combine_ffn")
    combine(3)
    layer_out[...] = (summed_s[...] + gn_s[...]).astype(BF16)

    mark("gain_wait")
    each(1, nlang, lambda i: gainl_copy(lax.rem(me + i, nlang), lax.rem(me + i, nlang)).wait_recv())
    grad_gain[...] = jnp.sum(gain_l[...], axis=0)

    mark("wait_out")
    mark("wait_sent")
    def sent_ctx(i):
        p = lax.rem(c + i, nctx)
        for n in range(4):
            in_copy(n, p, c).wait_send()
        rcopy(attsend.at[at(p * T, T)], att.at[:, at(c * HD, HD)], att_ss.at[p], att_rs.at[c], {"ctx": p}).wait_send()
        gr_copy(p, c, p).wait_send()
        gain_copy(p, c).wait_send()
        for n in (0, 2):
            go_copy(n, triples[n][0], triples[n][1], p, c).wait_send()

    loop(1, nctx, sent_ctx)

    def sent_lang(d):
        for phase in range(4):
            rcopy(
                msg_s.at[phase, at(d * MR, MR)],
                msg_r.at[phase, at(d * MR, MR)],
                lang_ss.at[phase, d],
                lang_rs.at[phase, d],
                {"lang": lax.rem(me + d, nlang)},
            ).wait_send()
        gainl_copy(lax.rem(me + d, nlang), me).wait_send()

    loop(1, nlang, sent_lang)

    for w, buf in ((0, rows_g), (1, rows_n)):
        for g in range(GROUPS):
            for side in range(2):
                near_copy(w, buf, g, side).wait_send()
                half_copy(w, buf, g, side).wait_send()
                mid_copy(w, g, side).wait_send()
                for h in range(2):
                    fin_copy(w, g, side, h).wait_send()
            for what in range(5):
                sib_copy(w, buf, g, what).wait_send()

    def sent_pair(i):
        for w in range(2):
            for g in range(GROUPS):
                pair_copy(w, i, g).wait_send()

    loop(0, X, sent_pair)
    for copy in own_out:
        copy.wait()
    for copy in out_w:
        copy.wait()
    def wait_out(i):
        p = lax.rem(c + i, nctx)
        for n, (src, dst) in enumerate(triples):
            go_copy(n, src, dst, p, p).wait_recv()

    each(1, nctx, wait_out)

    each(1, nctx, lambda i: go_copy(1, gksend, gk_hbm, lax.rem(c + i, nctx), c).wait_send())
    mark(None)


def store(*refs):
    n = (len(refs) - 2) // 3
    fetch_sem, store_sem = refs[-2:]
    fetches = [pltpu.make_async_copy(refs[i], refs[2 * n + i], fetch_sem.at[i]) for i in range(n)]
    stores = [pltpu.make_async_copy(refs[2 * n + i], refs[n + i], store_sem.at[i]) for i in range(n)]
    for copy in fetches:
        copy.start()
    for fetch, copy in zip(fetches, stores):
        fetch.wait()
        copy.start()
    for copy in stores:
        copy.wait()


def local(
    attn_queries,
    attn_keys,
    attn_values,
    residual,
    cotangent,
    segment_ids,
    language_ids,
    token_counts,
    norm_gain,
    gate_weight,
    up_weight,
    down_weight,
):
    nctx = lax.axis_size("ctx")
    nlang = lax.axis_size("lang")
    T, D = attn_queries.shape[1:]
    F = gate_weight.shape[2]
    L = nctx * T
    J = D // HD
    X = nctx // 2
    MR = PITCH * J
    LG = nlang // GROUPS
    RG = LG * CAP
    BR = nlang * CAP
    R = nctx * BR
    vmem = lambda *shape: pltpu.VMEM(shape, BF16)
    vmem32 = lambda *shape: pltpu.VMEM(shape, F32)
    dma = lambda *shape: pltpu.SemaphoreType.DMA(shape)
    scratch = [
        vmem(L, HD),
        vmem(L, HD),
        vmem(L, HD),
        vmem(16, T),
        vmem(16, L),
        vmem32(L, T),
        vmem32(nctx * L, T),
        vmem(L, L),
        vmem(HD, L),
        vmem(L, HD),
        vmem(T, D),
        vmem(D, F),
        vmem(D, F),
        vmem(F, D),
        vmem(D, F),
        vmem(D, F),
        vmem(F, D),
        vmem32(T, D),
        vmem32(T, D),
        vmem32(T, D),
        vmem32(T, D),
        vmem(J * T, HD),
        vmem(nlang * MR, J * T),
        vmem(J * T, nlang * MR),
        vmem(J * RG, LG * MR),
        vmem(LG * MR, J * 128),
        vmem(J * 128, HD),
        vmem(4, nlang * MR, HD),
        vmem(4, nlang * MR, HD),
        vmem(R, D),
        vmem(R, D),
        vmem32(R, F),
        vmem(R, F),
        vmem(R, F),
        vmem(R, F),
        vmem(2, R, D),
        vmem(2, X * BR, D),
        vmem(2, X * BR, D),
        vmem(2, BR, D),
        vmem(2, 2 * BR, D),
        vmem(T, D),
        vmem(L, HD),
        vmem(L, HD),
        vmem(L, HD),
        vmem(L, HD),
        vmem32(J, HD),
        vmem32(nctx, J, HD),
        vmem32(J, HD),
        vmem32(nlang, J, HD),
        dma(6),
        dma(3),
        dma(4, nctx),
        dma(4, nctx),
        dma(nctx),
        dma(nctx),
        dma(4, nlang),
        dma(4, nlang),
        dma(2 * GROUPS, 2),
        dma(2 * GROUPS, 2),
        dma(2 * GROUPS, 2),
        dma(2 * GROUPS, 2),
        dma(2 * GROUPS, 5),
        dma(2 * GROUPS, 5),
        dma(2, X * GROUPS),
        dma(2, X * GROUPS),
        dma(2 * GROUPS, 2),
        dma(2 * GROUPS, 2),
        dma(2 * GROUPS, 4),
        dma(2 * GROUPS, 4),
        dma(nctx),
        dma(nctx),
        dma(3, nctx),
        dma(3, nctx),
        dma(nctx),
        dma(nctx),
        dma(nlang),
        dma(nlang),
    ]
    anywhere = pl.BlockSpec(memory_space=pl.ANY)
    inside = pl.BlockSpec(memory_space=pltpu.VMEM)
    shape = lambda *dims: jax.ShapeDtypeStruct(dims, BF16)
    outs = pl.pallas_call(
        functools.partial(kernel, nctx, nlang),
        out_shape=(
            shape(T, D),
            shape(T, D),
            shape(T, D),
            shape(T, D),
            shape(T, D),
            jax.ShapeDtypeStruct((J, HD), F32),
            shape(D, F),
            shape(D, F),
            shape(F, D),
        ),
        in_specs=[anywhere] * 3 + [inside] * 6 + [anywhere] * 3,
        out_specs=(inside, anywhere, anywhere, anywhere, inside, inside, anywhere, anywhere, anywhere),
        scratch_shapes=scratch,
        compiler_params=pltpu.CompilerParams(collective_id=0, has_side_effects=True, vmem_limit_bytes=62 * 1024 * 1024),
        cost_estimate=pl.CostEstimate(flops=16_000_000_000, bytes_accessed=10_000_000, transcendentals=3_000_000),
        name="layer",
    )(
        attn_queries[0],
        attn_keys[0],
        attn_values[0],
        residual[0],
        cotangent[0],
        segment_ids,
        language_ids.reshape(1, T),
        token_counts.reshape(1, nlang),
        norm_gain.reshape(1, D),
        gate_weight[0],
        up_weight[0],
        down_weight[0],
    )
    outs = pl.pallas_call(
        store,
        out_shape=tuple(jax.ShapeDtypeStruct(o.shape, o.dtype) for o in outs),
        in_specs=[anywhere] * len(outs),
        out_specs=(anywhere,) * len(outs),
        scratch_shapes=[pltpu.VMEM(o.shape, o.dtype) for o in outs] + [dma(len(outs)), dma(len(outs))],
        compiler_params=pltpu.CompilerParams(vmem_limit_bytes=58 * 1024 * 1024),
        name="store",
    )(*outs)
    layer_out, gq, gk, gv, gres, ggain, gwg, gwu, gwd = outs
    return (
        layer_out[None],
        gq[None],
        gk[None],
        gv[None],
        gres[None],
        ggain.reshape(D),
        gwg[None],
        gwu[None],
        gwd[None],
    )


def solution(mesh):
    block = P("lang", "ctx", None)
    in_specs = (
        block,
        block,
        block,
        block,
        block,
        P("lang", "ctx"),
        block,
        P(),
        P(),
        P("lang", None, "ctx"),
        P("lang", None, "ctx"),
        block,
    )
    out_specs = (
        block,
        block,
        block,
        block,
        block,
        P(),
        P("lang", None, "ctx"),
        P("lang", None, "ctx"),
        block,
    )
    return jax.shard_map(local, mesh=mesh, in_specs=in_specs, out_specs=out_specs, check_vma=False)
```

```python
import functools

import jax
import jax.numpy as jnp
from jax import lax
from jax.experimental import pallas as pl
from jax.experimental.pallas import tpu as pltpu
from jax.sharding import PartitionSpec as P

HD = 128
EPSILON = 1e-06
CAP = 5
PITCH = 6
GROUPS = 2
MESH = pl.DeviceIdType.MESH
F32 = jnp.float32
BF16 = jnp.bfloat16
MASKED = -1e30


def dot_nn(a, b):
    return lax.dot_general(a, b, (((1,), (0,)), ((), ())), preferred_element_type=F32)


def dot_nt(a, b):
    return lax.dot_general(a, b, (((1,), (1,)), ((), ())), preferred_element_type=F32)


def at(start, size, step=None):
    return pl.ds(pl.multiple_of(start, step or size), size)


def kernel(
    nctx,
    nlang,
    q_hbm,
    k_hbm,
    v_hbm,
    residual,
    cotangent,
    segment,
    language,
    counts,
    gain,
    wg_hbm,
    wu_hbm,
    wd_hbm,
    layer_out,
    gq_hbm,
    gk_hbm,
    gv_hbm,
    grad_res,
    grad_gain,
    gwg_hbm,
    gwu_hbm,
    gwd_hbm,
    qh,
    kh,
    vh,
    segsend,
    segrow,
    segcol,
    probs_t,
    probs_h,
    kh_t,
    attsend,
    att,
    wg,
    wu,
    wd,
    gwg,
    gwu,
    gwd,
    summed_s,
    normed_s,
    gout_s,
    gn_s,
    stack,
    sel,
    sel_t,
    spread,
    spread_t,
    stack_r,
    msg_s,
    msg_r,
    rows_n,
    rows_g,
    gh_s,
    hid_s,
    ggp_s,
    gup_s,
    part,
    pair_r,
    sum_s,
    mid_r,
    fin_r,
    grsend,
    grh,
    gqsend,
    gksend,
    gvsend,
    gain_s,
    gain_c,
    gain_l_s,
    gain_l,
    loc_sem,
    out_sem,
    in_s,
    in_r,
    att_ss,
    att_rs,
    lang_ss,
    lang_rs,
    near_ss,
    near_rs,
    half_ss,
    half_rs,
    sib_ss,
    sib_rs,
    pair_ss,
    pair_rs,
    mid_ss,
    mid_rs,
    fin_ss,
    fin_rs,
    gr_ss,
    gr_rs,
    go_ss,
    go_rs,
    gain_ss,
    gain_rs,
    gainl_ss,
    gainl_rs,
):
    T, D = residual.shape
    L = nctx * T
    J = D // HD
    X = nctx // 2
    assert X == 4
    F = wg.shape[1]
    H = D // 2
    MR = PITCH * J
    LG = nlang // GROUPS
    RG = LG * CAP
    OP = 128
    scale = HD ** (-0.5)
    c = lax.axis_index("ctx")
    me = lax.axis_index("lang")
    x = c // 2
    core = c % 2
    sib = x * 2 + 1 - core
    right, left, across = (x + 1) % X, (x + 3) % X, (x + 2) % X

    def rcopy(src, dst, ssem, rsem, dev):
        return pltpu.make_async_remote_copy(
            src_ref=src, dst_ref=dst, send_sem=ssem, recv_sem=rsem, device_id=dev, device_id_type=MESH
        )

    def each(lo, hi, body):
        for i in range(lo, hi):
            body(i)

    def loop(lo, hi, body, unroll=1):
        def step(i, carry):
            body(i)
            return carry

        lax.fori_loop(lo, hi, step, 0, unroll=unroll)

    scope = []

    def mark(name):
        if scope:
            scope.pop().__exit__(None, None, None)
        if name:
            scope.append(jax.named_scope(name))
            scope[-1].__enter__()

    mark("entry")
    weight_in = [
        pltpu.make_async_copy(src, dst, loc_sem.at[i])
        for i, (src, dst) in enumerate(((wd_hbm, wd), (wg_hbm, wg), (wu_hbm, wu)))
    ]
    own_in = [
        pltpu.make_async_copy(src.at[:, at(c * HD, HD)], dst.at[at(c * T, T)], loc_sem.at[3 + i])
        for i, (src, dst) in enumerate(((k_hbm, kh), (q_hbm, qh), (v_hbm, vh)))
    ]
    segsend[...] = jnp.broadcast_to(segment[...].astype(F32), segsend.shape).astype(BF16)

    barrier = pltpu.get_barrier_semaphore()
    loop(1, nctx, lambda i: pl.semaphore_signal(barrier, inc=1, device_id={"ctx": lax.rem(c + i, nctx)}, device_id_type=MESH))
    loop(1, nlang, lambda i: pl.semaphore_signal(barrier, inc=1, device_id={"lang": lax.rem(me + i, nlang)}, device_id_type=MESH))
    for copy in own_in:
        copy.start()
    pl.semaphore_wait(barrier, nctx - 1 + nlang - 1)

    mark("send_qkv")
    def in_copy(i, to, owner):
        if i == 3:
            src, dst = segsend, segrow.at[:, at(owner * T, T)]
        else:
            src, dst = ((k_hbm, kh), (q_hbm, qh), (v_hbm, vh))[i]
            src, dst = src.at[:, at(to * HD, HD)], dst.at[at(owner * T, T)]
        return rcopy(src, dst, in_s.at[i, to], in_r.at[i, owner], {"ctx": to})

    for which in ((3, 0), (1,), (2,)):

        def send_in(i):
            for n in which:
                in_copy(n, lax.rem(c + i, nctx), c).start()

        each(1, nctx, send_in)
    for copy in weight_in:
        copy.start()
    segrow[:, at(c * T, T)] = segsend[...]

    mark("slots")
    lang_row = language[...].astype(F32)
    lang_col = jnp.transpose(jnp.broadcast_to(lang_row, (T, T)))
    earlier = lax.broadcasted_iota(jnp.int32, (T, T), 0) < lax.broadcasted_iota(jnp.int32, (T, T), 1)
    rank = jnp.sum(jnp.where((lang_col == lang_row) & earlier, 1.0, 0.0), axis=0, keepdims=True)
    slot_row = lang_row * float(MR) + rank
    slot_col = jnp.transpose(jnp.broadcast_to(slot_row, (T, T)))[:, 0:1].astype(jnp.int32)
    slot_row = slot_row.astype(jnp.int32)
    for j in range(J):
        hit = lax.broadcasted_iota(jnp.int32, (nlang * MR, T), 0) == slot_row + PITCH * j
        sel[:, j * T : (j + 1) * T] = jnp.where(hit, 1.0, 0.0).astype(BF16)

    lang_hit = lang_col[:, 0:1] == lax.broadcasted_iota(jnp.int32, (T, nlang), 1).astype(F32)
    count = jnp.sum(jnp.where(lang_hit, counts[...].astype(F32), 0.0), axis=1, keepdims=True)
    gout_s[...] = cotangent[...].astype(F32) * (16.0 * lax.rsqrt(count))

    NY = 4 if nlang % 8 == 0 else 1
    NZ = nlang // NY
    me_z, me_y = lax.div(me, NY), lax.rem(me, NY)

    def partner(d, sign):
        if NY == 1:
            return lax.rem(me + nlang + sign * d, nlang)
        turn_z = d // NY
        off_z = (2 * turn_z) % NZ + turn_z // (NZ // 2)
        return lax.rem(me_z + NZ + sign * off_z, NZ) * NY + lax.rem(me_y + NY + sign * (d % NY), NY)

    def dispatch(phase, stacked):
        for j in range(J):
            stack[j * T : (j + 1) * T, :] = stacked[:, j * HD : (j + 1) * HD]
        msg_s[phase] = dot_nn(sel[...], stack[...]).astype(BF16)

        def one(d):
            to = partner(d, 1)
            rcopy(
                msg_s.at[phase, at(to * MR, MR)],
                msg_r.at[phase, at(d * MR, MR)],
                lang_ss.at[phase, d],
                lang_rs.at[phase, d],
                {"lang": to},
            ).start()

        each(1, nlang, one)
        msg_r[phase, 0:MR, :] = msg_s[phase, at(me * MR, MR), :]

    def lang_wait(phase, lo, hi):
        def one(d):
            rcopy(
                msg_s.at[phase, at(d * MR, MR)],
                msg_r.at[phase, at(d * MR, MR)],
                lang_ss.at[phase, d],
                lang_rs.at[phase, d],
                {"lang": me},
            ).wait_recv()

        each(lo, hi, one)

    def lang_wait_but_own(phase):
        def one(d):
            l = lax.rem(me + d, nlang)
            rcopy(
                msg_s.at[phase, at(l * MR, MR)],
                msg_r.at[phase, at(l * MR, MR)],
                lang_ss.at[phase, d],
                lang_rs.at[phase, l],
                {"lang": me},
            ).wait_recv()

        each(1, nlang, one)

    mark("dispatch_grads")
    dispatch(0, gout_s[...].astype(BF16))

    mark("spread")
    o_col = lax.broadcasted_iota(jnp.int32, (RG, LG * MR), 0)
    base = ((o_col * 205) >> 10) * (MR - CAP) + o_col
    for j in range(J):
        hit = lax.broadcasted_iota(jnp.int32, (RG, LG * MR), 1) == base + PITCH * j
        spread[j * RG : (j + 1) * RG, :] = jnp.where(hit, 1.0, 0.0).astype(BF16)

    mark("wait_qkv")
    for copy in own_in:
        copy.wait()

    def wait_in(n):
        each(1, nctx, lambda i: in_copy(n, lax.rem(c + i, nctx), lax.rem(c + i, nctx)).wait_recv())

    for n in (3, 0):
        wait_in(n)
    for p in range(nctx):
        row = segrow[0:1, p * T : (p + 1) * T].astype(F32)
        segcol[p * T : (p + 1) * T, :] = jnp.transpose(jnp.broadcast_to(row, (T, T)))

    mark("attention")
    def forward(i):
        p = lax.rem(c + nctx - i, nctx)
        s = dot_nt(qh[at(p * T, T), :], kh[...]) * scale
        same = segcol[at(p * T, T), 0:1] == segrow[0:1, :].astype(F32)
        s = jnp.where(same, s, MASKED)
        e = jnp.exp(s - jnp.max(s, axis=1, keepdims=True))
        probs_h[at(p * T, T), :] = (e / jnp.sum(e, axis=1, keepdims=True)).astype(BF16)

    def wait_query(i):
        p = lax.rem(c + nctx - i, nctx)
        in_copy(1, p, p).wait_recv()

    BATCH = nctx // 2
    for first in range(0, nctx, BATCH):
        each(max(1, first), first + BATCH, wait_query)
        loop(first, first + BATCH, forward, BATCH)
    mark("wait_values")
    wait_in(2)
    mark("attended")

    attsend[...] = dot_nn(probs_h[...], vh[...]).astype(BF16)

    def send_attended(i):
        p = lax.rem(c + i, nctx)
        rcopy(attsend.at[at(p * T, T)], att.at[:, at(c * HD, HD)], att_ss.at[p], att_rs.at[c], {"ctx": p}).start()

    each(1, nctx, send_attended)
    att[:, at(c * HD, HD)] = attsend[at(c * T, T), :]

    def block(chip, g, k):
        return at(((chip * GROUPS + g) * 2 + k) * RG, RG, 16)

    def near_copy(w, buf, g, side):
        rows = block(x, g, core)
        to = (right, left)[side] * 2 + core
        n = w * GROUPS + g
        return rcopy(buf.at[rows], buf.at[rows], near_ss.at[n, side], near_rs.at[n, side], {"ctx": to})

    def half_copy(w, buf, g, side):
        rows = block((left, right)[side], g, core)
        cols = slice(side * H, (side + 1) * H)
        to = (right, left)[side] * 2 + core
        n = w * GROUPS + g
        return rcopy(buf.at[rows, cols], buf.at[rows, cols], half_ss.at[n, side], half_rs.at[n, side], {"ctx": to})

    def sib_copy(w, buf, g, what, k=core):
        n = w * GROUPS + g
        rows = block((x, left, right, across, across)[what], g, k)
        cols = slice(None) if what < 3 else slice((what - 3) * H, (what - 2) * H)
        return rcopy(buf.at[rows, cols], buf.at[rows, cols], sib_ss.at[n, what], sib_rs.at[n, what], {"ctx": sib})

    def gather_send(w, buf, phase, g):
        lang_wait(phase, max(1, g * LG), (g + 1) * LG)
        rows = block(x, g, core)
        for j in range(J):
            buf[rows, j * HD : (j + 1) * HD] = dot_nn(
                spread[j * RG : (j + 1) * RG, :], msg_r[phase, g * LG * MR : (g + 1) * LG * MR, :]
            ).astype(BF16)
        near_copy(w, buf, g, 0).start()
        near_copy(w, buf, g, 1).start()
        sib_copy(w, buf, g, 0).start()

    def near_forward(w, buf, g):
        for side in range(2):
            rows = block((left, right)[side], g, core)
            n = w * GROUPS + g
            rcopy(buf.at[rows], buf.at[rows], near_ss.at[n, side], near_rs.at[n, side], {"ctx": sib}).wait_recv()
            half_copy(w, buf, g, side).start()
            sib_copy(w, buf, g, 1 + side).start()

    def half_forward(w, buf, g):
        for side in range(2):
            rows = block(across, g, core)
            cols = slice(side * H, (side + 1) * H)
            n = w * GROUPS + g
            rcopy(
                buf.at[rows, cols], buf.at[rows, cols], half_ss.at[n, side], half_rs.at[n, side], {"ctx": sib}
            ).wait_recv()
            sib_copy(w, buf, g, 3 + side).start()

    def sib_wait(w, buf, g, what):
        sib_copy(w, buf, g, what, 1 - core).wait_recv()

    mark("grad_rows")
    for g in range(GROUPS):
        gather_send(0, rows_g, 0, g)

    mark("wait_attended")
    def wait_att(i):
        p = lax.rem(c + i, nctx)
        rcopy(attsend.at[at(p * T, T)], att.at[:, at(p * HD, HD)], att_ss.at[p], att_rs.at[p], {"ctx": p}).wait_recv()

    each(1, nctx, wait_att)
    mark("norm_dispatch")
    summed = residual[...].astype(F32) + att[...].astype(F32)
    summed_s[...] = summed
    inv_rms = lax.rsqrt(jnp.mean(summed * summed, axis=1, keepdims=True) + EPSILON)
    normed = summed * inv_rms
    normed_s[...] = normed
    dispatch(1, (normed * gain[...]).astype(BF16))

    mark("layouts")
    for j in range(J):
        hit = lax.broadcasted_iota(jnp.int32, (T, nlang * MR), 1) == slot_col + PITCH * j
        sel_t[j * T : (j + 1) * T, :] = jnp.where(hit, 1.0, 0.0).astype(BF16)
    o_row = lax.broadcasted_iota(jnp.int32, (LG * MR, OP), 1)
    base_row = ((o_row * 205) >> 10) * (MR - CAP) + o_row
    inside = o_row < RG
    for j in range(J):
        hit = (lax.broadcasted_iota(jnp.int32, (LG * MR, OP), 0) == base_row + PITCH * j) & inside
        spread_t[:, j * OP : (j + 1) * OP] = jnp.where(hit, 1.0, 0.0).astype(BF16)
    stack_r[...] = jnp.zeros_like(stack_r)

    mark("back_probs")

    def back_probs(p):
        s = dot_nt(kh[...], qh[at(p * T, T), :]) * scale
        same = segcol[...] == segrow[0:1, at(p * T, T)].astype(F32)
        s = jnp.where(same, s, MASKED)
        e = jnp.exp(s - jnp.max(s, axis=0, keepdims=True))
        probs = e / jnp.sum(e, axis=0, keepdims=True)
        probs_t[at(p * L, L), :] = probs
        probs_h[:, at(p * T, T)] = probs.astype(BF16)

    loop(0, nctx, back_probs, BATCH)
    kh_t[...] = jnp.transpose(kh[...])
    mark("forward_grads")
    for g in range(GROUPS):
        near_forward(0, rows_g, g)
    mark("grad_hidden")
    weight_in[0].wait()
    CR = GROUPS * 2 * RG
    for g in range(GROUPS):
        for what in range(3):
            sib_wait(0, rows_g, g, what)

    def grad_hidden(i):
        rows = at((x + i + i // 2 - 2 * (i // 3)) % X * CR, CR, 16)
        gh_s[rows, :] = dot_nt(rows_g[rows, :], wd[...])

    loop(0, X - 1, grad_hidden)
    mark("norm_rows")
    for g in range(GROUPS):
        gather_send(1, rows_n, 1, g)
        half_forward(0, rows_g, g)
    weight_in[1].wait()
    weight_in[2].wait()

    FT = min(F, 256)
    DT = min(D, 512)

    def flat(chip, g):
        return at((chip * GROUPS + g) * RG, RG, 16)

    def pair_copy(w, chip, g):
        n = chip * GROUPS + g
        return rcopy(
            part.at[w, block(chip, g, 1 - core)], pair_r.at[w, flat(chip, g)], pair_ss.at[w, n], pair_rs.at[w, n], {"ctx": sib}
        )

    def pair_sum(w, chip, g, cols):
        own = part[w, block(chip, g, core), cols].astype(F32)
        return own + pair_r[w, flat(chip, g), cols].astype(F32)

    halves = (slice(0, H), slice(H, D))

    def mid_copy(w, g, h):
        to = (right, left)[h] * 2 + core
        src = sum_s.at[w, flat(across, g), halves[h]]
        n = w * GROUPS + g
        return rcopy(src, mid_r.at[w, at(g * RG, RG, 16), halves[h]], mid_ss.at[n, h], mid_rs.at[n, h], {"ctx": to})

    def fin_copy(w, g, side, h):
        chip = (right, left)[side]
        src = sum_s.at[w, flat(chip, g), halves[h]]
        dst = fin_r.at[w, at((side * GROUPS + g) * RG, RG, 16), halves[h]]
        n = w * GROUPS + g
        return rcopy(src, dst, fin_ss.at[n, side * 2 + h], fin_rs.at[n, side * 2 + h], {"ctx": chip * 2 + core})

    def sum_across(w, g):
        pair_copy(w, across, g).wait_recv()
        for h in range(2):
            sum_s[w, flat(across, g), halves[h]] = pair_sum(w, across, g, halves[h]).astype(BF16)
            mid_copy(w, g, h).start()

    def sum_near(w, g, side):
        chip, h = (right, left)[side], 1 - side
        pair_copy(w, chip, g).wait_recv()
        sum_s[w, flat(chip, g), halves[h]] = pair_sum(w, chip, g, halves[h]).astype(BF16)
        fin_copy(w, g, side, h).start()

    def sum_late(w, g):
        for side in range(2):
            chip, h = (right, left)[side], side
            mid_copy(w, g, h).wait_recv()
            total = pair_sum(w, chip, g, halves[h]) + mid_r[w, at(g * RG, RG, 16), halves[h]].astype(F32)
            sum_s[w, flat(chip, g), halves[h]] = total.astype(BF16)
            fin_copy(w, g, side, h).start()

    def sum_own(w, g):
        pair_copy(w, x, g).wait_recv()
        for side in range(2):
            for h in range(2):
                fin_copy(w, g, side, h).wait_recv()
        total = pair_sum(w, x, g, slice(None))
        for side in range(2):
            total = total + fin_r[w, at((side * GROUPS + g) * RG, RG, 16), :].astype(F32)
        return total.astype(BF16)

    def feed(rows):
        for n in range(F // FT):
            cols = slice(n * FT, (n + 1) * FT)
            pre_gate = dot_nn(rows_n[rows, :], wg[:, cols])
            pre_up = dot_nn(rows_n[rows, :], wu[:, cols])
            gh = gh_s[rows, cols]
            sig = jax.nn.sigmoid(pre_gate)
            silu = pre_gate * sig
            hid_s[rows, cols] = (silu * pre_up).astype(BF16)
            ggp_s[rows, cols] = (gh * pre_up * sig * (1.0 + pre_gate * (1.0 - sig))).astype(BF16)
            gup_s[rows, cols] = (gh * silu).astype(BF16)
        for n in range(D // DT):
            cols = slice(n * DT, (n + 1) * DT)
            part[0, rows, cols] = (dot_nt(ggp_s[rows, :], wg[cols, :]) + dot_nt(gup_s[rows, :], wu[cols, :])).astype(BF16)

    def feed_chip(i):
        chip = (x + i + i // 2) % X
        for g in range(GROUPS):
            for what, when in ((0, 0), (2, 1), (1, 2)):

                @pl.when(i == when)
                def _():
                    sib_wait(1, rows_n, g, what)

        feed(at(chip * CR, CR, 16))
        for g in range(GROUPS):
            pair_copy(0, chip, g).start()

    mark("feed_own")
    loop(0, 1, feed_chip)
    mark("feed_near_wait")
    for g in range(GROUPS):
        near_forward(1, rows_n, g)
    mark("feed_near")
    loop(1, 3, feed_chip)
    mark("sum_near")
    for g in range(GROUPS):
        for side in range(2):
            sum_near(0, g, side)
    for g in range(GROUPS):
        half_forward(1, rows_n, g)
    for g in range(GROUPS):
        for what in (3, 4):
            sib_wait(0, rows_g, g, what)
    loop(X - 1, X, grad_hidden)
    mark("feed_across")

    def feed_across(g):
        for m in range(GROUPS):

            @pl.when(g == m)
            def _():
                sib_wait(1, rows_n, m, 3)
                sib_wait(1, rows_n, m, 4)

        feed(at((across * GROUPS + g) * 2 * RG, 2 * RG, 16))
        pair_copy(0, across, g).start()

    loop(0, GROUPS, feed_across)
    mark("sum_across")
    for g in range(GROUPS):
        sum_across(0, g)

    mark("down")

    def down(i):
        rows = at(i * CR, CR, 16)
        part[1, rows, :] = dot_nn(hid_s[rows, :], wd[...]).astype(BF16)
        for g in range(GROUPS):
            pair_copy(1, i, g).start()

    loop(0, X, down)
    mark("sum_late")
    for g in range(GROUPS):
        sum_late(0, g)

    def grad_w(n):
        cols = at(n * FT, FT)
        turned = jnp.transpose(rows_n[:, cols])
        gwg[cols, :] = dot_nn(turned, ggp_s[...]).astype(BF16)
        gwu[cols, :] = dot_nn(turned, gup_s[...]).astype(BF16)

    def grad_wd(n):
        cols = at(n * FT, FT)
        gwd[cols, :] = dot_nn(jnp.transpose(hid_s[:, cols]), rows_g[...]).astype(BF16)

    def return_send(w, phase):
        for g in range(GROUPS):
            total = sum_own(w, g)
            for j in range(J):
                stack_r[j * OP : j * OP + RG, :] = total[:, j * HD : (j + 1) * HD]
            msg_s[phase, g * LG * MR : (g + 1) * LG * MR, :] = dot_nn(spread_t[...], stack_r[...]).astype(BF16)

            def one(d):
                to = partner(d, -1)
                rcopy(
                    msg_s.at[phase, at(d * MR, MR)],
                    msg_r.at[phase, at(me * MR, MR)],
                    lang_ss.at[phase, d],
                    lang_rs.at[phase, me],
                    {"lang": to},
                ).start()

            each(max(1, g * LG), (g + 1) * LG, one)
        msg_r[phase, at(me * MR, MR), :] = msg_s[phase, 0:MR, :]

    def combine(phase):
        lang_wait_but_own(phase)
        for j in range(J):
            gn_s[:, j * HD : (j + 1) * HD] = dot_nn(sel_t[j * T : (j + 1) * T, :], msg_r[phase])

    mark("grad_w_a")
    half = max(1, (D // FT) // 2)
    loop(0, half, grad_w)
    mark("return_grads")
    return_send(0, 2)
    mark("ffn_sums")
    for g in range(GROUPS):
        sum_across(1, g)
    for g in range(GROUPS):
        for side in range(2):
            sum_near(1, g, side)
    mark("grad_w_b")
    loop(half, D // FT, grad_w)
    mark("ffn_late")
    for g in range(GROUPS):
        sum_late(1, g)
    mark("grad_wd")
    out_w = [
        pltpu.make_async_copy(src, dst, out_sem.at[i])
        for i, (src, dst) in enumerate(((gwg, gwg_hbm), (gwu, gwu_hbm), (gwd, gwd_hbm)))
    ]
    out_w[0].start()
    out_w[1].start()
    wd_half = F // FT // 2
    loop(0, wd_half, grad_wd)

    mark("combine_grads")
    combine(2)
    mark("grad_residual")
    grad_normin = gn_s[...]
    normed = normed_s[...]
    summed = summed_s[...]
    inv_rms = lax.rsqrt(jnp.mean(summed * summed, axis=1, keepdims=True) + EPSILON)
    scaled = grad_normin * gain[...]
    gres = gout_s[...] + inv_rms * (scaled - normed * jnp.mean(scaled * normed, axis=1, keepdims=True))
    grsend[...] = gres.astype(BF16)

    def gr_copy(to, owner, sem_at):
        return rcopy(grsend.at[:, at(to * HD, HD)], grh.at[at(owner * T, T)], gr_ss.at[sem_at], gr_rs.at[owner], {"ctx": to})

    each(1, nctx, lambda i: gr_copy(lax.rem(c + i, nctx), c, lax.rem(c + i, nctx)).start())
    grh[at(c * T, T), :] = grsend[:, at(c * HD, HD)]
    grad_res[...] = grsend[...]
    gain_part = jnp.sum(grad_normin * normed, axis=0, keepdims=True)
    for j in range(J):
        gain_s[j : j + 1, :] = gain_part[:, j * HD : (j + 1) * HD]

    def gain_copy(to, owner):
        return rcopy(gain_s, gain_c.at[owner], gain_ss.at[to], gain_rs.at[owner], {"ctx": to})

    each(1, nctx, lambda i: gain_copy(lax.rem(c + i, nctx), c).start())
    gain_c[c] = gain_s[...]

    mark("return_ffn")
    return_send(1, 3)
    loop(wd_half, F // FT, grad_wd)
    out_w[2].start()

    mark("backward")
    def go_copy(n, src, dst, to, owner):
        return rcopy(src.at[at(to * T, T)], dst.at[:, at(owner * HD, HD)], go_ss.at[n, to], go_rs.at[n, owner], {"ctx": to})

    each(1, nctx, lambda i: gr_copy(lax.rem(c + i, nctx), lax.rem(c + i, nctx), lax.rem(c + i, nctx)).wait_recv())
    mark("grad_values")
    gvsend[...] = dot_nn(probs_h[...], grh[...]).astype(BF16)
    each(1, nctx, lambda i: go_copy(2, gvsend, gv_hbm, lax.rem(c + i, nctx), c).start())
    mark("gain")

    each(1, nctx, lambda i: gain_copy(lax.rem(c + i, nctx), lax.rem(c + i, nctx)).wait_recv())
    gain_l_s[...] = jnp.sum(gain_c[...], axis=0)

    def gainl_copy(to, owner):
        return rcopy(gain_l_s, gain_l.at[owner], gainl_ss.at[to], gainl_rs.at[owner], {"lang": to})

    each(1, nlang, lambda i: gainl_copy(lax.rem(me + i, nlang), me).start())
    gain_l[me] = gain_l_s[...]
    mark("backward_loop")

    def backward(i):
        p = lax.rem(c + 1 + i, nctx)
        probs = probs_t[at(p * L, L), :]
        gp = dot_nt(vh[...], grh[at(p * T, T), :])
        gs = (probs * (gp - jnp.sum(probs * gp, axis=0, keepdims=True))).astype(BF16)
        probs_h[:, at(p * T, T)] = gs
        gqsend[at(p * T, T), :] = jnp.transpose(dot_nn(kh_t[...], gs) * scale).astype(BF16)

        @pl.when(i < nctx - 1)
        def _():
            go_copy(0, gqsend, gq_hbm, p, c).start()

    loop(0, nctx, backward, BATCH)
    mark("send_keys")
    gksend[...] = (dot_nn(probs_h[...], qh[...]) * scale).astype(BF16)
    each(1, nctx, lambda i: go_copy(1, gksend, gk_hbm, lax.rem(c + i, nctx), c).start())
    triples = ((gqsend, gq_hbm), (gksend, gk_hbm), (gvsend, gv_hbm))
    own_out = [
        pltpu.make_async_copy(src.at[at(c * T, T)], dst.at[:, at(c * HD, HD)], loc_sem.at[3 + n])
        for n, (src, dst) in enumerate(triples)
    ]
    for copy in own_out:
        copy.start()

    mark("combine_ffn")
    combine(3)
    layer_out[...] = (summed_s[...] + gn_s[...]).astype(BF16)

    mark("gain_wait")
    each(1, nlang, lambda i: gainl_copy(lax.rem(me + i, nlang), lax.rem(me + i, nlang)).wait_recv())
    grad_gain[...] = jnp.sum(gain_l[...], axis=0)

    mark("wait_out")
    mark("wait_sent")
    def sent_ctx(i):
        p = lax.rem(c + i, nctx)
        for n in range(4):
            in_copy(n, p, c).wait_send()
        rcopy(attsend.at[at(p * T, T)], att.at[:, at(c * HD, HD)], att_ss.at[p], att_rs.at[c], {"ctx": p}).wait_send()
        gr_copy(p, c, p).wait_send()
        gain_copy(p, c).wait_send()
        for n in (0, 2):
            go_copy(n, triples[n][0], triples[n][1], p, c).wait_send()

    loop(1, nctx, sent_ctx)

    def sent_lang(d):
        for phase in range(4):
            rcopy(
                msg_s.at[phase, at(d * MR, MR)],
                msg_r.at[phase, at(d * MR, MR)],
                lang_ss.at[phase, d],
                lang_rs.at[phase, d],
                {"lang": lax.rem(me + d, nlang)},
            ).wait_send()
        gainl_copy(lax.rem(me + d, nlang), me).wait_send()

    loop(1, nlang, sent_lang)

    for w, buf in ((0, rows_g), (1, rows_n)):
        for g in range(GROUPS):
            for side in range(2):
                near_copy(w, buf, g, side).wait_send()
                half_copy(w, buf, g, side).wait_send()
                mid_copy(w, g, side).wait_send()
                for h in range(2):
                    fin_copy(w, g, side, h).wait_send()
            for what in range(5):
                sib_copy(w, buf, g, what).wait_send()

    def sent_pair(i):
        for w in range(2):
            for g in range(GROUPS):
                pair_copy(w, i, g).wait_send()

    loop(0, X, sent_pair)
    for copy in own_out:
        copy.wait()
    for copy in out_w:
        copy.wait()
    def wait_out(i):
        p = lax.rem(c + i, nctx)
        for n, (src, dst) in enumerate(triples):
            go_copy(n, src, dst, p, p).wait_recv()

    each(1, nctx, wait_out)

    each(1, nctx, lambda i: go_copy(1, gksend, gk_hbm, lax.rem(c + i, nctx), c).wait_send())
    mark(None)


def store(*refs):
    n = (len(refs) - 2) // 3
    fetch_sem, store_sem = refs[-2:]
    fetches = [pltpu.make_async_copy(refs[i], refs[2 * n + i], fetch_sem.at[i]) for i in range(n)]
    stores = [pltpu.make_async_copy(refs[2 * n + i], refs[n + i], store_sem.at[i]) for i in range(n)]
    for copy in fetches:
        copy.start()
    for fetch, copy in zip(fetches, stores):
        fetch.wait()
        copy.start()
    for copy in stores:
        copy.wait()


def local(
    attn_queries,
    attn_keys,
    attn_values,
    residual,
    cotangent,
    segment_ids,
    language_ids,
    token_counts,
    norm_gain,
    gate_weight,
    up_weight,
    down_weight,
):
    nctx = lax.axis_size("ctx")
    nlang = lax.axis_size("lang")
    T, D = attn_queries.shape[1:]
    F = gate_weight.shape[2]
    L = nctx * T
    J = D // HD
    X = nctx // 2
    MR = PITCH * J
    LG = nlang // GROUPS
    RG = LG * CAP
    BR = nlang * CAP
    R = nctx * BR
    vmem = lambda *shape: pltpu.VMEM(shape, BF16)
    vmem32 = lambda *shape: pltpu.VMEM(shape, F32)
    dma = lambda *shape: pltpu.SemaphoreType.DMA(shape)
    scratch = [
        vmem(L, HD),
        vmem(L, HD),
        vmem(L, HD),
        vmem(16, T),
        vmem(16, L),
        vmem32(L, T),
        vmem32(nctx * L, T),
        vmem(L, L),
        vmem(HD, L),
        vmem(L, HD),
        vmem(T, D),
        vmem(D, F),
        vmem(D, F),
        vmem(F, D),
        vmem(D, F),
        vmem(D, F),
        vmem(F, D),
        vmem32(T, D),
        vmem32(T, D),
        vmem32(T, D),
        vmem32(T, D),
        vmem(J * T, HD),
        vmem(nlang * MR, J * T),
        vmem(J * T, nlang * MR),
        vmem(J * RG, LG * MR),
        vmem(LG * MR, J * 128),
        vmem(J * 128, HD),
        vmem(4, nlang * MR, HD),
        vmem(4, nlang * MR, HD),
        vmem(R, D),
        vmem(R, D),
        vmem32(R, F),
        vmem(R, F),
        vmem(R, F),
        vmem(R, F),
        vmem(2, R, D),
        vmem(2, X * BR, D),
        vmem(2, X * BR, D),
        vmem(2, BR, D),
        vmem(2, 2 * BR, D),
        vmem(T, D),
        vmem(L, HD),
        vmem(L, HD),
        vmem(L, HD),
        vmem(L, HD),
        vmem32(J, HD),
        vmem32(nctx, J, HD),
        vmem32(J, HD),
        vmem32(nlang, J, HD),
        dma(6),
        dma(3),
        dma(4, nctx),
        dma(4, nctx),
        dma(nctx),
        dma(nctx),
        dma(4, nlang),
        dma(4, nlang),
        dma(2 * GROUPS, 2),
        dma(2 * GROUPS, 2),
        dma(2 * GROUPS, 2),
        dma(2 * GROUPS, 2),
        dma(2 * GROUPS, 5),
        dma(2 * GROUPS, 5),
        dma(2, X * GROUPS),
        dma(2, X * GROUPS),
        dma(2 * GROUPS, 2),
        dma(2 * GROUPS, 2),
        dma(2 * GROUPS, 4),
        dma(2 * GROUPS, 4),
        dma(nctx),
        dma(nctx),
        dma(3, nctx),
        dma(3, nctx),
        dma(nctx),
        dma(nctx),
        dma(nlang),
        dma(nlang),
    ]
    anywhere = pl.BlockSpec(memory_space=pl.ANY)
    inside = pl.BlockSpec(memory_space=pltpu.VMEM)
    shape = lambda *dims: jax.ShapeDtypeStruct(dims, BF16)
    outs = pl.pallas_call(
        functools.partial(kernel, nctx, nlang),
        out_shape=(
            shape(T, D),
            shape(T, D),
            shape(T, D),
            shape(T, D),
            shape(T, D),
            jax.ShapeDtypeStruct((J, HD), F32),
            shape(D, F),
            shape(D, F),
            shape(F, D),
        ),
        in_specs=[anywhere] * 3 + [inside] * 6 + [anywhere] * 3,
        out_specs=(inside, anywhere, anywhere, anywhere, inside, inside, anywhere, anywhere, anywhere),
        scratch_shapes=scratch,
        compiler_params=pltpu.CompilerParams(collective_id=0, has_side_effects=True, vmem_limit_bytes=62 * 1024 * 1024),
        cost_estimate=pl.CostEstimate(flops=16_000_000_000, bytes_accessed=10_000_000, transcendentals=3_000_000),
        name="layer",
    )(
        attn_queries[0],
        attn_keys[0],
        attn_values[0],
        residual[0],
        cotangent[0],
        segment_ids,
        language_ids.reshape(1, T),
        token_counts.reshape(1, nlang),
        norm_gain.reshape(1, D),
        gate_weight[0],
        up_weight[0],
        down_weight[0],
    )
    outs = pl.pallas_call(
        store,
        out_shape=tuple(jax.ShapeDtypeStruct(o.shape, o.dtype) for o in outs),
        in_specs=[anywhere] * len(outs),
        out_specs=(anywhere,) * len(outs),
        scratch_shapes=[pltpu.VMEM(o.shape, o.dtype) for o in outs] + [dma(len(outs)), dma(len(outs))],
        compiler_params=pltpu.CompilerParams(vmem_limit_bytes=58 * 1024 * 1024),
        name="store",
    )(*outs)
    layer_out, gq, gk, gv, gres, ggain, gwg, gwu, gwd = outs
    return (
        layer_out[None],
        gq[None],
        gk[None],
        gv[None],
        gres[None],
        ggain.reshape(D),
        gwg[None],
        gwu[None],
        gwd[None],
    )


def solution(mesh):
    block = P("lang", "ctx", None)
    in_specs = (
        block,
        block,
        block,
        block,
        block,
        P("lang", "ctx"),
        block,
        P(),
        P(),
        P("lang", None, "ctx"),
        P("lang", None, "ctx"),
        block,
    )
    out_specs = (
        block,
        block,
        block,
        block,
        block,
        P(),
        P("lang", None, "ctx"),
        P("lang", None, "ctx"),
        block,
    )
    return jax.shard_map(local, mesh=mesh, in_specs=in_specs, out_specs=out_specs, check_vma=False)
```
